32 devices in a mesh: layers: 2 (over y), expert: 16 (over z, x, core).
Axes of the slice: x: 2, y: 2, z: 4, core: 2. Of those that a mesh axis runs over, the one named last changes fastest.
Arguments:
- gate_codes: bfloat16 [32, 2048, 768], P(('layers', 'expert')), parts along dimension 0, may hold values from -4 to 4
- up_codes: bfloat16 [32, 2048, 768], P(('layers', 'expert')), parts along dimension 0, may hold values from -4 to 4
- gate_scale: bfloat16 [32, 16, 6], P(('layers', 'expert')), parts along dimension 0, may hold values from 0.25 to 4
- up_scale: bfloat16 [32, 16, 6], P(('layers', 'expert')), parts along dimension 0, may hold values from 0.25 to 4
- pairs: int32 [16, 2], P('layers'), parts along dimension 0, may hold values from 0 to 15, as said below
- counts: int32 [32], P('layers'), parts along dimension 0, may hold values from 64 to 1023
- unit_order: int32 [16, 768], P('layers'), parts along dimension 0, may hold values from 0 to 767, each once within a row
- owners: int32 [96, 1], P('layers'), parts along dimension 0, may hold values from 0 to 15; in each aligned block of 48 rows (0 to 47, 48 to 95, ...) at most 6 rows name the same one
Outputs:
- merged: bfloat16 [192, 256, 2048], P(('layers', 'expert')), parts along dimension 0
- similarity: float32 [16, 768], P('layers'), parts along dimension 0
The draws below stay inside these ranges and needn't reach their ends.
There are 2 independent parts, one for each index of `layers`. The reference program is written for one: setup_inputs(seed, part) draws one part's arguments, and reference() takes and returns one part's arrays. A program takes and returns all parts, laid end to end along the dimension named above; each array names one. Nothing has to cross between parts.
Inputs may be any that keep to these rules, and one draw needn't show every extreme that they name: `pairs`: every expert appears in exactly one pair. `owners`: at most 6 pieces have the same owner, and some owner has exactly 6.
All inputs are finite; a program needn't handle non-finite values.
Results may differ from the reference program's by a relative error of at most 0.005.
Values may be sent and summed in bfloat16 or wider, within the bound.
No kernel may reach another device: no remote copies, remote signals or barrier semaphores. Data moves between devices by JAX's collectives and lax.ppermute only.
A program may use at most 128 MiB of HBM per device.

```python
import math
import jax
import jax.numpy as jnp
import numpy as np
from jax import lax

D = 2048
FF = 768
BLK = 128
U = 128
CAP = 6
EXPERTS = 16
PAIRS = 8
PIECES = 48


def draw_pairs(key, part):
    key = jax.random.fold_in(key, 11)
    shuffled = jax.random.permutation(key, EXPERTS)
    return shuffled.astype(jnp.int32).reshape(PAIRS, 2)


def touch_ends(values, rng, smallest, largest):
    place = [jax.random.randint(jax.random.fold_in(rng, axis), (), 0, length) for axis, length in enumerate(values.shape)]
    longest = values.shape.index(max(values.shape))
    beside = place[:longest] + [(place[longest] + 1) % values.shape[longest]] + place[longest + 1:]
    return values.at[tuple(place)].set(smallest).at[tuple(beside)].set(largest)


def block_levels(own_key, shape, cuts, low, top_value):
    gain = 1.0
    for position, blocks in cuts:
        steps = jax.random.uniform(jax.random.fold_in(jax.random.fold_in(own_key, 6), position), (blocks,), jnp.float32, low / len(cuts), top_value / len(cuts))
        gain = gain * jnp.repeat(jnp.exp(steps), shape[position] // blocks).reshape((-1,) + (1,) * (len(shape) - 1 - position))
    return gain


def deal_out(rng, own, number, rows, amount, top, reach, lean):
    sequence = jax.random.permutation(rng, amount)
    crowded, usual = shares(amount, rows * top, reach, lean, True), shares(amount, rows * top, reach, lean, False)
    places = jnp.arange(amount)

    def named(tallies, turn):
        used = int((tallies > 0).sum())
        fixed = max(1, used // 4)
        shifted = fixed + (places - fixed + turn * (used - fixed)) % max(1, amount - fixed)
        return jnp.zeros((amount,), jnp.int32).at[sequence[jnp.where(places < fixed, places, shifted)]].set(jnp.asarray(tallies, jnp.int32))

    tallies = jnp.where(number % 4 == 0, named(crowded, number // 4), named(usual, number - number // 4 - 1))
    mixed = jax.random.permutation(jax.random.fold_in(own, 3), amount)
    giver, receiver = mixed[0:amount // 2 * 2:2], mixed[1:amount // 2 * 2:2]
    room = jnp.minimum(tallies[giver] - 1, reach - tallies[receiver]) // 2
    room = jnp.where((giver == sequence[0]) | (receiver == sequence[0]) | (tallies[receiver] == 0), 0, jnp.maximum(room, 0))
    shifted = jax.random.randint(jax.random.fold_in(own, 4), (amount // 2,), 0, 1 << 20) % (room + 1)
    tallies = tallies.at[giver].add(-shifted).at[receiver].add(shifted)
    members = jnp.searchsorted(jnp.cumsum(tallies), jnp.arange(rows * top), side="right").astype(jnp.int32)
    listing = members.reshape(top, rows).T
    listing = listing[jax.random.permutation(jax.random.fold_in(own, 1), rows)]
    turn = jax.random.randint(jax.random.fold_in(own, 2), (rows, 1), 0, top)
    return jnp.take_along_axis(listing, (jnp.arange(top)[None, :] + turn) % top, axis=1)


def shares(amount, total, most, skew, full):
    weights = [(1 << 20) // math.isqrt(standing ** skew) + 1 for standing in range(1, amount + 1)]
    largest = most if full else min(most, max(-(-total // amount), total * weights[0] // sum(weights)))
    least = 1 if total - largest >= amount - 1 else 0
    holding, surplus = [largest] + [least] * (amount - 1), total - largest - least * (amount - 1)
    while surplus > 0:
        free = [i for i in range(1, amount) if holding[i] < largest] or [i for i in range(1, amount) if holding[i] < most]
        pool, left = sum([weights[i] for i in free]), surplus
        for i in free:
            more = min(most - holding[i], max(1, left * weights[i] // pool), surplus)
            holding[i] = holding[i] + more
            surplus = surplus - more
    return np.array(holding)


def centred(own_key, dims, scale, limit, split=(), dtype=jnp.bfloat16):
    drawn = scale * jax.random.normal(own_key, dims, jnp.float32)
    if split:
        drawn = drawn * block_levels(own_key, dims, split, -0.22, 0.18)
    return jnp.clip(drawn, -limit, limit).astype(dtype)


def setup_inputs(seed: int = 0, part: int = 0) -> dict:
    streams_of = jax.random.split(jax.random.key(seed), 9)
    part_keys = jax.random.split(jax.random.fold_in(streams_of[8], part), 9)
    gate_codes = centred(part_keys[0], (EXPERTS, D, FF), 1.0, 4.0, ((0, 16),))
    up_codes = centred(part_keys[1], (EXPERTS, D, FF), 1.0, 4.0, ((0, 16),))
    gate_scale = jnp.clip(jnp.exp(math.log(4.0) - 2.7725887 * jax.random.uniform(part_keys[2], (EXPERTS, D // BLK, FF // BLK), jnp.float32) ** block_levels(part_keys[2], (EXPERTS, D // BLK, FF // BLK), ((0, 16),), -0.2, 0.2)), 0.25, 4.0).astype(jnp.bfloat16)
    up_scale = jnp.clip(jnp.exp(math.log(4.0) - 2.7725887 * jax.random.uniform(part_keys[3], (EXPERTS, D // BLK, FF // BLK), jnp.float32) ** block_levels(part_keys[3], (EXPERTS, D // BLK, FF // BLK), ((0, 16),), -0.2, 0.2)), 0.25, 4.0).astype(jnp.bfloat16)
    pairs = draw_pairs(jax.random.fold_in(jax.random.fold_in(streams_of[8], part), 71), part)
    counts = touch_ends(jax.random.randint(part_keys[5], (EXPERTS,), 64, 1024), jax.random.fold_in(part_keys[5], 1), 64, 1023).astype(jnp.int32)
    unit_order = jax.vmap(lambda own: jax.random.permutation(own, FF))(jax.random.split(part_keys[6], PAIRS)).reshape((PAIRS, FF)).astype(jnp.int32)
    owners_keys = jax.random.split(jax.random.fold_in(part_keys[7], 1), PIECES // PIECES)
    owners_turns = jax.random.permutation(jax.random.fold_in(part_keys[7], 3), PIECES // PIECES)
    owners = jax.vmap(lambda own, number: deal_out(jax.random.fold_in(part_keys[7], 2), own, number, PIECES, EXPERTS, 1, CAP, 2))(owners_keys, owners_turns).reshape((PIECES, 1))
    return {"gate_codes": gate_codes, "up_codes": up_codes, "gate_scale": gate_scale, "up_scale": up_scale, "pairs": pairs, "counts": counts, "unit_order": unit_order, "owners": owners}


epsilon = 1e-06

def dequantize(codes, scale):
    spread = jnp.repeat(jnp.repeat(scale.astype(jnp.float32), BLK, axis=0), BLK, axis=1)
    return (codes.astype(jnp.float32) * spread).astype(jnp.bfloat16)

def slot_rows(owners):
    owner_ids = owners[:, 0].astype(jnp.int32)
    count = owner_ids.shape[0]
    matches = owner_ids[:, None] == owner_ids[None, :]
    earlier = jnp.arange(count)[None, :] < jnp.arange(count)[:, None]
    slot_rank = lax.optimization_barrier(jnp.sum(jnp.where(matches & earlier, 1, 0), axis=1)).astype(jnp.int32)
    return (owner_ids * CAP + slot_rank).astype(jnp.int32)

def reference(gate_codes, up_codes, gate_scale, up_scale, pairs, counts, unit_order, owners):
    gate_values = lax.map(lambda item: dequantize(item[0], item[1]), (gate_codes, gate_scale))
    up_values = lax.map(lambda item: dequantize(item[0], item[1]), (up_codes, up_scale))
    scale_factor = math.sqrt(2.0 * D)

    def one_pair(item):
        pair, order = item
        left_gate = gate_values[pair[0]].astype(jnp.float32)
        left_up = up_values[pair[0]].astype(jnp.float32)
        right_gate = jnp.take(gate_values[pair[1]], order, axis=1).astype(jnp.float32)
        right_up = jnp.take(up_values[pair[1]], order, axis=1).astype(jnp.float32)
        intersection = lax.optimization_barrier(jnp.sum(left_gate * right_gate + left_up * right_up, axis=0))
        left_norm = lax.optimization_barrier(jnp.sum(left_gate * left_gate + left_up * left_up, axis=0))
        right_norm = lax.optimization_barrier(jnp.sum(right_gate * right_gate + right_up * right_up, axis=0))
        similarity = intersection * scale_factor / jnp.sqrt((left_norm + epsilon) * (right_norm + epsilon))
        left_freq = counts[pair[0]].astype(jnp.float32)
        right_freq = counts[pair[1]].astype(jnp.float32)
        share = right_freq * jax.nn.sigmoid(similarity)
        total = left_freq + share
        merged_gate = ((left_freq * left_gate + share * right_gate) / total).astype(jnp.bfloat16)
        merged_up = ((left_freq * left_up + share * right_up) / total).astype(jnp.bfloat16)
        joined = jnp.stack((merged_gate, merged_up), axis=-1)
        joined = joined.reshape(D, FF // U, 2 * U).transpose(1, 2, 0)
        return (similarity, joined)
    similarity, joined = lax.map(one_pair, (pairs, unit_order))
    pieces = joined.reshape(PIECES, 2 * U, D)
    merged = jnp.zeros((EXPERTS * CAP, 2 * U, D), jnp.bfloat16).at[slot_rows(owners)].set(pieces)
    return (merged, similarity)
```

```python
import functools
import math

import jax
import jax.numpy as jnp
from jax import lax
from jax.experimental import pallas as pl
from jax.experimental.pallas import tpu as pltpu
from jax.sharding import PartitionSpec as P

BLK = 128
U = 128
CAP = 6
EPSILON = 1e-06
VMEM = 48 * 1024 * 1024


def slot_rows(owners):
    owner_ids = owners[:, 0]
    count = owner_ids.shape[0]
    matches = owner_ids[:, None] == owner_ids[None, :]
    earlier = jnp.arange(count)[None, :] < jnp.arange(count)[:, None]
    slot_rank = jnp.sum(jnp.where(matches & earlier, 1, 0), axis=1).astype(jnp.int32)
    return owner_ids * CAP + slot_rank


def own_order(pairs, unit_order, width):
    device_id = lax.axis_index("expert")
    is_right = pairs[:, 1] == device_id
    picked = jnp.sum(jnp.where(is_right[:, None], unit_order, 0), axis=0)
    identity = jnp.arange(width, dtype=jnp.int32)
    return jnp.where(jnp.any(is_right), picked, identity)


def prepare_kernel(source_ref, gate_ref, up_ref, gate_scale_ref, up_scale_ref, out_ref, select_ref):
    units = select_ref.shape[1]
    rows = gate_ref.shape[0]

    @pl.when(pl.program_id(0) == 0)
    def _():
        columns = lax.broadcasted_iota(jnp.int32, select_ref.shape, 1)
        select_ref[...] = (source_ref[...] == columns).astype(jnp.float32).astype(jnp.bfloat16)

    for kind, (codes_ref, scale_ref) in enumerate(
        ((gate_ref, gate_scale_ref), (up_ref, up_scale_ref))
    ):
        parts = []
        for block in range(rows // BLK):
            scale = scale_ref[0, block : block + 1, :]
            codes = codes_ref[block * BLK : (block + 1) * BLK, :].astype(jnp.float32)
            parts.append((codes * scale).astype(jnp.bfloat16))
        values = jnp.concatenate(parts, axis=0)
        chosen = lax.dot_general(
            select_ref[...], values, (((1,), (1,)), ((), ())), preferred_element_type=jnp.float32
        ).astype(jnp.bfloat16)
        out_ref[:, kind] = chosen.reshape(out_ref.shape[0], out_ref.shape[2], rows)


def prepare(source, gate_codes, up_codes, gate_scale, up_scale, devices):
    depth, units = gate_codes.shape
    per_device = units // devices
    tile = 256
    blocks = tile // BLK
    spread = lambda scale: jnp.repeat(scale.astype(jnp.float32), BLK, axis=1).reshape(
        depth // tile, blocks, units
    )
    return pl.pallas_call(
        prepare_kernel,
        grid=(depth // tile,),
        in_specs=[
            pl.BlockSpec((units, 1), lambda d: (0, 0)),
            pl.BlockSpec((tile, units), lambda d: (d, 0)),
            pl.BlockSpec((tile, units), lambda d: (d, 0)),
            pl.BlockSpec((1, blocks, units), lambda d: (d, 0, 0)),
            pl.BlockSpec((1, blocks, units), lambda d: (d, 0, 0)),
        ],
        out_specs=pl.BlockSpec((devices, 2, per_device, tile), lambda d: (0, 0, 0, d)),
        out_shape=jax.ShapeDtypeStruct((devices, 2, per_device, depth), jnp.bfloat16),
        scratch_shapes=[pltpu.VMEM((units, units), jnp.bfloat16)],
        compiler_params=pltpu.CompilerParams(vmem_limit_bytes=VMEM),
        name="prepare",
    )(source[:, None], gate_codes, up_codes, spread(gate_scale), spread(up_scale))


def merge_kernel(
    pairs_ref, counts_ref, slots_ref, left_ref, right_ref, similarity_ref, out_ref, ready, sems
):
    pair = pl.program_id(0)
    pair_count = pl.num_programs(0)
    per_device, depth = left_ref.shape[2], left_ref.shape[3]
    pieces, piece_rows = ready.shape[1], ready.shape[2]
    left_gate = left_ref[0, 0].astype(jnp.float32)
    left_up = left_ref[0, 1].astype(jnp.float32)
    right_gate = right_ref[0, 0].astype(jnp.float32)
    right_up = right_ref[0, 1].astype(jnp.float32)
    total_of = lambda value: jnp.sum(value, axis=1, keepdims=True)
    intersection = total_of(left_gate * right_gate + left_up * right_up)
    left_norm = total_of(left_gate * left_gate + left_up * left_up)
    right_norm = total_of(right_gate * right_gate + right_up * right_up)
    similarity = (
        intersection
        * math.sqrt(2.0 * depth)
        / jnp.sqrt((left_norm + EPSILON) * (right_norm + EPSILON))
    )
    similarity_ref[0] = similarity
    left_freq = counts_ref[pairs_ref[2 * pair]].astype(jnp.float32)
    right_freq = counts_ref[pairs_ref[2 * pair + 1]].astype(jnp.float32)
    share = right_freq * jax.nn.sigmoid(similarity)
    total = left_freq + share
    left_weight = left_freq / total
    right_weight = share / total
    merged = jnp.concatenate(
        (
            left_weight * left_gate + right_weight * right_gate,
            left_weight * left_up + right_weight * right_up,
        ),
        axis=0,
    ).astype(jnp.bfloat16)
    to_row = lax.broadcasted_iota(jnp.int32, (2 * per_device, 2 * per_device), 0)
    from_row = lax.broadcasted_iota(jnp.int32, (2 * per_device, 2 * per_device), 1)
    weave = from_row == jnp.right_shift(to_row, 1) + per_device * jnp.bitwise_and(to_row, 1)
    woven = jnp.dot(
        weave.astype(jnp.float32).astype(jnp.bfloat16), merged, preferred_element_type=jnp.float32
    )
    slot = lax.rem(pair, 2)

    def copies(which_pair, which_slot):
        return [
            pltpu.make_async_copy(
                ready.at[which_slot, piece],
                out_ref.at[slots_ref[which_pair * pieces + piece]],
                sems.at[which_slot, piece],
            )
            for piece in range(pieces)
        ]

    @pl.when(pair >= 2)
    def _():
        for copy in copies(pair - 2, slot):
            copy.wait()

    ready[slot] = woven.astype(jnp.bfloat16).reshape(pieces, piece_rows, depth)
    for copy in copies(pair, slot):
        copy.start()

    @pl.when(pair == pair_count - 1)
    def _():
        for copy in copies(pair - 1, 1 - slot):
            copy.wait()
        for copy in copies(pair, slot):
            copy.wait()


def merge(pairs, counts, slots, rows, devices):
    _, _, per_device, depth = rows.shape
    pair_count = pairs.shape[0]
    pieces = slots.shape[0] // pair_count
    piece_rows = 2 * per_device // pieces
    grid_spec = pltpu.PrefetchScalarGridSpec(
        num_scalar_prefetch=3,
        grid=(pair_count,),
        in_specs=[
            pl.BlockSpec((1, 2, per_device, depth), lambda p, pairs, *_: (pairs[2 * p], 0, 0, 0)),
            pl.BlockSpec(
                (1, 2, per_device, depth), lambda p, pairs, *_: (pairs[2 * p + 1], 0, 0, 0)
            ),
        ],
        out_specs=[
            pl.BlockSpec((1, per_device, 1), lambda p, *_: (p, 0, 0)),
            pl.BlockSpec(memory_space=pl.ANY),
        ],
        scratch_shapes=[
            pltpu.VMEM((2, pieces, piece_rows, depth), jnp.bfloat16),
            pltpu.SemaphoreType.DMA((2, pieces)),
        ],
    )
    return pl.pallas_call(
        merge_kernel,
        grid_spec=grid_spec,
        out_shape=[
            jax.ShapeDtypeStruct((pair_count, per_device, 1), jnp.float32),
            jax.ShapeDtypeStruct((devices * CAP, piece_rows, depth), jnp.bfloat16),
        ],
        compiler_params=pltpu.CompilerParams(vmem_limit_bytes=VMEM),
        name="merge",
    )(pairs.reshape(-1), counts, slots, rows, rows)


def place_kernel(filled_ref, in_ref, out_ref):
    value = in_ref[:, 0].reshape(out_ref.shape[1], out_ref.shape[2])
    keep = pl.program_id(0) < filled_ref[0]
    out_ref[0] = jnp.where(keep, value, jnp.zeros_like(value))


def place(filled, arrived):
    devices, cap, piece_rows, depth = arrived.shape
    grid_spec = pltpu.PrefetchScalarGridSpec(
        num_scalar_prefetch=1,
        grid=(cap,),
        in_specs=[pl.BlockSpec((devices, 1, piece_rows, depth), lambda s, *_: (0, s, 0, 0))],
        out_specs=pl.BlockSpec((1, devices * piece_rows, depth), lambda s, *_: (s, 0, 0)),
    )
    return pl.pallas_call(
        place_kernel,
        grid_spec=grid_spec,
        out_shape=jax.ShapeDtypeStruct((cap, devices * piece_rows, depth), arrived.dtype),
        compiler_params=pltpu.CompilerParams(vmem_limit_bytes=VMEM),
        name="place",
    )(filled, arrived)


def body(gate_codes, up_codes, gate_scale, up_scale, pairs, counts, unit_order, owners):
    devices = lax.axis_size("expert")
    units = gate_codes.shape[2]
    pieces = units // U
    share_units = U // devices
    per_device = pieces * share_units
    order = own_order(pairs, unit_order, units)
    source = order.reshape(pieces, devices, share_units).transpose(1, 0, 2).reshape(units)
    outgoing = prepare(
        source, gate_codes[0], up_codes[0], gate_scale[0], up_scale[0], devices
    )
    rows = lax.all_to_all(outgoing, "expert", split_axis=0, concat_axis=0, tiled=True)
    similarity_part, merged = merge(pairs, counts, slot_rows(owners), rows, devices)
    pair_count = pairs.shape[0]
    merged = merged.reshape(devices, CAP, merged.shape[1], merged.shape[2])
    arrived = lax.all_to_all(merged, "expert", split_axis=0, concat_axis=0, tiled=True)
    similarity = lax.all_gather(similarity_part.reshape(1, -1), "expert", axis=0, tiled=True)
    similarity = similarity.reshape(devices, pair_count, pieces, share_units)
    similarity = similarity.transpose(1, 2, 0, 3).reshape(pair_count, units)
    filled = jnp.sum((owners[:, 0] == lax.axis_index("expert")).astype(jnp.int32))[None]
    return place(filled, arrived), similarity


def solution(mesh):
    in_specs = (
        P(("layers", "expert"), None, None),
        P(("layers", "expert"), None, None),
        P(("layers", "expert"), None, None),
        P(("layers", "expert"), None, None),
        P("layers", None),
        P("layers"),
        P("layers", None),
        P("layers", None),
    )
    out_specs = (P(("layers", "expert"), None, None), P("layers", None))
    return jax.shard_map(body, mesh=mesh, in_specs=in_specs, out_specs=out_specs, check_vma=False)
```

```python
import functools
import math

import jax
import jax.numpy as jnp
from jax import lax
from jax.experimental import pallas as pl
from jax.experimental.pallas import tpu as pltpu
from jax.sharding import PartitionSpec as P

BLK = 128
U = 128
CAP = 6
EPSILON = 1e-06
VMEM = 48 * 1024 * 1024


def own_order(pairs, unit_order, width):
    device_id = lax.axis_index("expert")
    is_right = pairs[:, 1] == device_id
    picked = jnp.sum(jnp.where(is_right[:, None], unit_order, 0), axis=0)
    identity = jnp.arange(width, dtype=jnp.int32)
    return jnp.where(jnp.any(is_right), picked, identity)


def prepare_kernel(source_ref, gate_ref, up_ref, gate_scale_ref, up_scale_ref, out_ref, select_ref):
    units = select_ref.shape[1]
    rows = gate_ref.shape[0]

    @pl.when(pl.program_id(0) == 0)
    def _():
        columns = lax.broadcasted_iota(jnp.int32, select_ref.shape, 1)
        select_ref[...] = (source_ref[...] == columns).astype(jnp.float32).astype(jnp.bfloat16)

    for kind, (codes_ref, scale_ref) in enumerate(
        ((gate_ref, gate_scale_ref), (up_ref, up_scale_ref))
    ):
        parts = []
        for block in range(rows // BLK):
            scale = scale_ref[0, block : block + 1, :]
            codes = codes_ref[block * BLK : (block + 1) * BLK, :].astype(jnp.float32)
            parts.append((codes * scale).astype(jnp.bfloat16))
        values = jnp.concatenate(parts, axis=0)
        chosen = lax.dot_general(
            select_ref[...], values, (((1,), (1,)), ((), ())), preferred_element_type=jnp.float32
        ).astype(jnp.bfloat16)
        out_ref[:, kind] = chosen.reshape(out_ref.shape[0], out_ref.shape[2], rows)


def prepare(source, gate_codes, up_codes, gate_scale, up_scale, devices):
    depth, units = gate_codes.shape
    per_device = units // devices
    tile = 256
    blocks = tile // BLK
    spread = lambda scale: jnp.repeat(scale.astype(jnp.float32), BLK, axis=1).reshape(
        depth // tile, blocks, units
    )
    return pl.pallas_call(
        prepare_kernel,
        grid=(depth // tile,),
        in_specs=[
            pl.BlockSpec((units, 1), lambda d: (0, 0)),
            pl.BlockSpec((tile, units), lambda d: (d, 0)),
            pl.BlockSpec((tile, units), lambda d: (d, 0)),
            pl.BlockSpec((1, blocks, units), lambda d: (d, 0, 0)),
            pl.BlockSpec((1, blocks, units), lambda d: (d, 0, 0)),
        ],
        out_specs=pl.BlockSpec((devices, 2, per_device, tile), lambda d: (0, 0, 0, d)),
        out_shape=jax.ShapeDtypeStruct((devices, 2, per_device, depth), jnp.bfloat16),
        scratch_shapes=[pltpu.VMEM((units, units), jnp.bfloat16)],
        compiler_params=pltpu.CompilerParams(vmem_limit_bytes=VMEM),
        name="prepare",
    )(source[:, None], gate_codes, up_codes, spread(gate_scale), spread(up_scale))


def merge_kernel(
    widths,
    pairs_ref,
    counts_ref,
    near_ref,
    place_ref,
    left_ref,
    right_ref,
    similarity_ref,
    near_out,
    *rest,
):
    far_outs, (ready, sems) = rest[: len(widths)], rest[len(widths) :]
    pair = pl.program_id(0)
    pair_count = pl.num_programs(0)
    per_device, depth = left_ref.shape[2], left_ref.shape[3]
    pieces, piece_rows = ready.shape[1], ready.shape[2]
    left_gate = left_ref[0, 0].astype(jnp.float32)
    left_up = left_ref[0, 1].astype(jnp.float32)
    right_gate = right_ref[0, 0].astype(jnp.float32)
    right_up = right_ref[0, 1].astype(jnp.float32)
    total_of = lambda value: jnp.sum(value, axis=1, keepdims=True)
    intersection = total_of(left_gate * right_gate + left_up * right_up)
    left_norm = total_of(left_gate * left_gate + left_up * left_up)
    right_norm = total_of(right_gate * right_gate + right_up * right_up)
    similarity = (
        intersection
        * math.sqrt(2.0 * depth)
        / jnp.sqrt((left_norm + EPSILON) * (right_norm + EPSILON))
    )
    similarity_ref[0] = similarity
    left_freq = counts_ref[pairs_ref[2 * pair]].astype(jnp.float32)
    right_freq = counts_ref[pairs_ref[2 * pair + 1]].astype(jnp.float32)
    share = right_freq * jax.nn.sigmoid(similarity)
    total = left_freq + share
    left_weight = left_freq / total
    right_weight = share / total
    merged = jnp.concatenate(
        (
            left_weight * left_gate + right_weight * right_gate,
            left_weight * left_up + right_weight * right_up,
        ),
        axis=0,
    ).astype(jnp.bfloat16)
    to_row = lax.broadcasted_iota(jnp.int32, (2 * per_device, 2 * per_device), 0)
    from_row = lax.broadcasted_iota(jnp.int32, (2 * per_device, 2 * per_device), 1)
    weave = from_row == jnp.right_shift(to_row, 1) + per_device * jnp.bitwise_and(to_row, 1)
    woven = jnp.dot(
        weave.astype(jnp.float32).astype(jnp.bfloat16), merged, preferred_element_type=jnp.float32
    )
    slot = lax.rem(pair, 2)

    def each_copy(which_pair, which_slot, act):
        for piece in range(pieces):
            index = which_pair * pieces + piece
            near = near_ref[index] == 1

            @pl.when(near)
            def _():
                act(
                    pltpu.make_async_copy(
                        ready.at[which_slot, piece],
                        near_out.at[place_ref[index]],
                        sems.at[which_slot, piece, 0],
                    )
                )

            @pl.when(jnp.logical_not(near))
            def _():
                begin = 0
                for chunk, width in enumerate(widths):
                    act(
                        pltpu.make_async_copy(
                            ready.at[which_slot, piece, :, pl.ds(begin, width)],
                            far_outs[chunk].at[place_ref[index]],
                            sems.at[which_slot, piece, chunk],
                        )
                    )
                    begin += width

    @pl.when(pair >= 2)
    def _():
        each_copy(pair - 2, slot, lambda copy: copy.wait())

    ready[slot] = woven.astype(jnp.bfloat16).reshape(pieces, piece_rows, depth)
    each_copy(pair, slot, lambda copy: copy.start())

    @pl.when(pair == pair_count - 1)
    def _():
        each_copy(pair - 1, 1 - slot, lambda copy: copy.wait())
        each_copy(pair, slot, lambda copy: copy.wait())


def merge(pairs, counts, near, places, rows, slots, listed, widths):
    _, _, per_device, depth = rows.shape
    pair_count = pairs.shape[0]
    pieces = near.shape[0] // pair_count
    piece_rows = 2 * per_device // pieces
    grid_spec = pltpu.PrefetchScalarGridSpec(
        num_scalar_prefetch=4,
        grid=(pair_count,),
        in_specs=[
            pl.BlockSpec((1, 2, per_device, depth), lambda p, pairs, *_: (pairs[2 * p], 0, 0, 0)),
            pl.BlockSpec(
                (1, 2, per_device, depth), lambda p, pairs, *_: (pairs[2 * p + 1], 0, 0, 0)
            ),
        ],
        out_specs=[pl.BlockSpec((1, per_device, 1), lambda p, *_: (p, 0, 0))]
        + [pl.BlockSpec(memory_space=pl.ANY)] * (1 + len(widths)),
        scratch_shapes=[
            pltpu.VMEM((2, pieces, piece_rows, depth), jnp.bfloat16),
            pltpu.SemaphoreType.DMA((2, pieces, len(widths))),
        ],
    )
    return pl.pallas_call(
        functools.partial(merge_kernel, widths),
        grid_spec=grid_spec,
        out_shape=[
            jax.ShapeDtypeStruct((pair_count, per_device, 1), jnp.float32),
            jax.ShapeDtypeStruct((slots, piece_rows, depth), jnp.bfloat16),
        ]
        + [jax.ShapeDtypeStruct((listed, piece_rows, width), jnp.bfloat16) for width in widths],
        compiler_params=pltpu.CompilerParams(vmem_limit_bytes=VMEM),
        name="merge",
    )(pairs.reshape(-1), counts, near, places, rows, rows)


def place_kernel(offset, filled_ref, in_ref, *rest):
    out_ref = rest[-1]
    value = in_ref[:, 0].reshape(out_ref.shape[1], out_ref.shape[2])
    keep = pl.program_id(0) < filled_ref[0]
    out_ref[0] = jnp.where(keep, value, jnp.zeros_like(value))


def place(filled, half, arrived, begin, depth, base=None):
    sources, cap, piece_rows, width = arrived.shape
    grid_spec = pltpu.PrefetchScalarGridSpec(
        num_scalar_prefetch=2,
        grid=(cap,),
        in_specs=[pl.BlockSpec((sources, 1, piece_rows, width), lambda s, *_: (0, s, 0, 0))]
        + ([] if base is None else [pl.BlockSpec(memory_space=pl.ANY)]),
        out_specs=pl.BlockSpec(
            (1, sources * piece_rows, width),
            lambda s, filled, half: (s, half[0], begin // width),
        ),
    )
    return pl.pallas_call(
        lambda filled_ref, half_ref, *refs: place_kernel(None, filled_ref, *refs),
        grid_spec=grid_spec,
        out_shape=jax.ShapeDtypeStruct((cap, 2 * sources * piece_rows, depth), arrived.dtype),
        input_output_aliases={} if base is None else {3: 0},
        compiler_params=pltpu.CompilerParams(vmem_limit_bytes=VMEM),
        name="place",
    )(filled, half, arrived, *(() if base is None else (base,)))


def body(gate_codes, up_codes, gate_scale, up_scale, pairs, counts, unit_order, owners):
    devices = lax.axis_size("expert")
    layers = lax.axis_size("layers")
    me = lax.axis_index("expert")
    depth, units = gate_codes.shape[1:]
    pieces = units // U
    share_units = U // devices
    per_device = pieces * share_units
    half = devices // 2
    side = me // half
    pair_count = pairs.shape[0]
    all_pieces = pair_count * pieces
    widths = (depth // 2, depth // 2)

    owner_ids = owners[:, 0]
    owner_side = owner_ids // half
    earlier = jnp.arange(all_pieces)[None, :] < jnp.arange(all_pieces)[:, None]
    count_earlier = lambda values: jnp.sum(
        jnp.where((values[:, None] == values[None, :]) & earlier, 1, 0), axis=1
    ).astype(jnp.int32)
    slot = (owner_ids % half) * CAP + count_earlier(owner_ids)
    position = count_earlier(owner_side)
    near = (owner_side == side).astype(jnp.int32)
    places = jnp.where(near == 1, slot, position)
    filled = jnp.sum((owner_ids == me).astype(jnp.int32))[None]
    from_list = jnp.sum(
        jnp.where(
            (jnp.arange(half * CAP)[:, None] == slot[None, :]) & (near == 1)[None, :],
            position[None, :],
            0,
        ),
        axis=1,
    ).astype(jnp.int32)
    ones = jnp.sum(owner_side).astype(jnp.int32)
    longest = jnp.maximum(ones, all_pieces - ones)
    for shift in range(1, layers):
        other = lax.ppermute(
            jnp.maximum(ones, all_pieces - ones),
            "layers",
            [(layer, (layer + shift) % layers) for layer in range(layers)],
        )
        longest = jnp.maximum(longest, other)
    least = all_pieces // 2
    sizes = [least + -(-least * part // 12) for part in (1, 2, 3, 6, 12)]
    level = sum((longest > size).astype(jnp.int32) for size in sizes[:-1])

    order = own_order(pairs, unit_order, units)
    source = order.reshape(pieces, devices, share_units).transpose(1, 0, 2).reshape(units)
    outgoing = prepare(
        source, gate_codes[0], up_codes[0], gate_scale[0], up_scale[0], devices
    )
    rows = lax.all_to_all(outgoing, "expert", split_axis=0, concat_axis=0, tiled=True)

    groups = [list(range(half)), list(range(half, devices))]
    mirror = [(device, (device + half) % devices) for device in range(devices)]

    def within_half(value):
        value = value.reshape(half, CAP, value.shape[1], value.shape[2])
        return lax.all_to_all(
            value, "expert", split_axis=0, concat_axis=0, tiled=True, axis_index_groups=groups
        )

    def deal(listed, rows, near, places, from_list):
        similarity_part, slots, *lists = merge(
            pairs, counts, near, places, rows, half * CAP, listed, widths
        )
        arrived = [within_half(slots)]
        for chunk in lists:
            chunk = lax.ppermute(chunk, "expert", mirror)
            spread = jnp.take(chunk, from_list, axis=0, mode="clip")
            spread, arrived[-1] = lax.optimization_barrier((spread, arrived[-1]))
            arrived.append(within_half(spread))
        similarity_part, _ = lax.optimization_barrier((similarity_part, spread))
        similarity = lax.all_gather(similarity_part.reshape(1, -1), "expert", axis=0, tiled=True)
        similarity = similarity.reshape(devices, pair_count, pieces, share_units)
        similarity = similarity.transpose(1, 2, 0, 3).reshape(pair_count, units)
        own, others = side.astype(jnp.int32)[None], (1 - side).astype(jnp.int32)[None]
        merged = place(filled, own, arrived[0], 0, depth)
        begin = 0
        for width, value in zip(widths, arrived[1:]):
            merged = place(filled, others, value, begin, depth, merged)
            begin += width
        return merged, similarity

    return lax.switch(
        level,
        [functools.partial(deal, size) for size in sizes],
        rows,
        near,
        places,
        from_list,
    )


def solution(mesh):
    in_specs = (
        P(("layers", "expert"), None, None),
        P(("layers", "expert"), None, None),
        P(("layers", "expert"), None, None),
        P(("layers", "expert"), None, None),
        P("layers", None),
        P("layers"),
        P("layers", None),
        P("layers", None),
    )
    out_specs = (P(("layers", "expert"), None, None), P("layers", None))
    return jax.shard_map(body, mesh=mesh, in_specs=in_specs, out_specs=out_specs, check_vma=False)
```

```python
import functools
import math

import jax
import jax.numpy as jnp
from jax import lax
from jax.experimental import pallas as pl
from jax.experimental.pallas import tpu as pltpu
from jax.sharding import PartitionSpec as P

BLK = 128
U = 128
CAP = 6
EPSILON = 1e-06
VMEM = 60 * 1024 * 1024
QUARTERS = 4
LIST_PARTS = (14, 15, 16, 17, 18, 20, 24)


def own_order(pairs, unit_order, width):
    device_id = lax.axis_index("expert")
    is_right = pairs[:, 1] == device_id
    picked = jnp.sum(jnp.where(is_right[:, None], unit_order, 0), axis=0)
    identity = jnp.arange(width, dtype=jnp.int32)
    return jnp.where(jnp.any(is_right), picked, identity)


def prepare_kernel(source_ref, gate_ref, up_ref, gate_scale_ref, up_scale_ref, out_ref, select_ref):
    units = select_ref.shape[1]
    rows = gate_ref.shape[0]

    @pl.when(pl.program_id(0) == 0)
    def _():
        columns = lax.broadcasted_iota(jnp.int32, select_ref.shape, 1)
        select_ref[...] = (source_ref[...] == columns).astype(jnp.float32).astype(jnp.bfloat16)

    for kind, (codes_ref, scale_ref) in enumerate(
        ((gate_ref, gate_scale_ref), (up_ref, up_scale_ref))
    ):
        parts = []
        for block in range(rows // BLK):
            scale = scale_ref[0, block : block + 1, :]
            codes = codes_ref[block * BLK : (block + 1) * BLK, :].astype(jnp.float32)
            parts.append((codes * scale).astype(jnp.bfloat16))
        values = jnp.concatenate(parts, axis=0)
        chosen = lax.dot_general(
            select_ref[...], values, (((1,), (1,)), ((), ())), preferred_element_type=jnp.float32
        ).astype(jnp.bfloat16)
        out_ref[:, kind] = chosen.reshape(out_ref.shape[0], out_ref.shape[2], rows)


def prepare(source, gate_codes, up_codes, gate_scale, up_scale, devices):
    depth, units = gate_codes.shape
    per_device = units // devices
    tile = 256
    blocks = tile // BLK
    spread = lambda scale: jnp.repeat(scale.astype(jnp.float32), BLK, axis=1).reshape(
        depth // tile, blocks, units
    )
    return pl.pallas_call(
        prepare_kernel,
        grid=(depth // tile,),
        in_specs=[
            pl.BlockSpec((units, 1), lambda d: (0, 0)),
            pl.BlockSpec((tile, units), lambda d: (d, 0)),
            pl.BlockSpec((tile, units), lambda d: (d, 0)),
            pl.BlockSpec((1, blocks, units), lambda d: (d, 0, 0)),
            pl.BlockSpec((1, blocks, units), lambda d: (d, 0, 0)),
        ],
        out_specs=pl.BlockSpec((devices, 2, per_device, tile), lambda d: (0, 0, 0, d)),
        out_shape=jax.ShapeDtypeStruct((devices, 2, per_device, depth), jnp.bfloat16),
        scratch_shapes=[pltpu.VMEM((units, units), jnp.bfloat16)],
        compiler_params=pltpu.CompilerParams(vmem_limit_bytes=VMEM),
        name="prepare",
    )(source[:, None], gate_codes, up_codes, spread(gate_scale), spread(up_scale))


def merge_kernel(
    pairs_ref, counts_ref, where_ref, place_ref, left_ref, right_ref, similarity_ref, *rest
):
    outs, (ready, sems) = rest[:-2], rest[-2:]
    pair = pl.program_id(0)
    pair_count = pl.num_programs(0)
    per_device, depth = left_ref.shape[2], left_ref.shape[3]
    pieces, piece_rows = ready.shape[1], ready.shape[2]
    left_gate = left_ref[0, 0].astype(jnp.float32)
    left_up = left_ref[0, 1].astype(jnp.float32)
    right_gate = right_ref[0, 0].astype(jnp.float32)
    right_up = right_ref[0, 1].astype(jnp.float32)
    total_of = lambda value: jnp.sum(value, axis=1, keepdims=True)
    intersection = total_of(left_gate * right_gate + left_up * right_up)
    left_norm = total_of(left_gate * left_gate + left_up * left_up)
    right_norm = total_of(right_gate * right_gate + right_up * right_up)
    similarity = (
        intersection
        * math.sqrt(2.0 * depth)
        / jnp.sqrt((left_norm + EPSILON) * (right_norm + EPSILON))
    )
    similarity_ref[0] = similarity
    left_freq = counts_ref[pairs_ref[2 * pair]].astype(jnp.float32)
    right_freq = counts_ref[pairs_ref[2 * pair + 1]].astype(jnp.float32)
    share = right_freq * jax.nn.sigmoid(similarity)
    total = left_freq + share
    left_weight = left_freq / total
    right_weight = share / total
    merged = jnp.concatenate(
        (
            left_weight * left_gate + right_weight * right_gate,
            left_weight * left_up + right_weight * right_up,
        ),
        axis=0,
    ).astype(jnp.bfloat16)
    to_row = lax.broadcasted_iota(jnp.int32, (2 * per_device, 2 * per_device), 0)
    from_row = lax.broadcasted_iota(jnp.int32, (2 * per_device, 2 * per_device), 1)
    weave = from_row == jnp.right_shift(to_row, 1) + per_device * jnp.bitwise_and(to_row, 1)
    woven = jnp.dot(
        weave.astype(jnp.float32).astype(jnp.bfloat16), merged, preferred_element_type=jnp.float32
    )
    slot = lax.rem(pair, 2)

    def each_copy(which_pair, which_slot, act):
        for piece in range(pieces):
            index = which_pair * pieces + piece
            for where, out_ref in enumerate(outs):

                @pl.when(where_ref[index] == where)
                def _():
                    act(
                        pltpu.make_async_copy(
                            ready.at[which_slot, piece],
                            out_ref.at[place_ref[index]],
                            sems.at[which_slot, piece],
                        )
                    )

    @pl.when(pair >= 2)
    def _():
        each_copy(pair - 2, slot, lambda copy: copy.wait())

    ready[slot] = woven.astype(jnp.bfloat16).reshape(pieces, piece_rows, depth)
    each_copy(pair, slot, lambda copy: copy.start())

    @pl.when(pair == pair_count - 1)
    def _():
        each_copy(pair - 1, 1 - slot, lambda copy: copy.wait())
        each_copy(pair, slot, lambda copy: copy.wait())


def merge(pairs, counts, where, places, rows, slots, listed):
    _, _, per_device, depth = rows.shape
    pair_count = pairs.shape[0]
    pieces = where.shape[0] // pair_count
    piece_rows = 2 * per_device // pieces
    lengths = (slots,) + (listed,) * (QUARTERS - 1)
    grid_spec = pltpu.PrefetchScalarGridSpec(
        num_scalar_prefetch=4,
        grid=(pair_count,),
        in_specs=[
            pl.BlockSpec((1, 2, per_device, depth), lambda p, pairs, *_: (pairs[2 * p], 0, 0, 0)),
            pl.BlockSpec(
                (1, 2, per_device, depth), lambda p, pairs, *_: (pairs[2 * p + 1], 0, 0, 0)
            ),
        ],
        out_specs=[pl.BlockSpec((1, per_device, 1), lambda p, *_: (p, 0, 0))]
        + [pl.BlockSpec(memory_space=pltpu.HBM)] * len(lengths),
        scratch_shapes=[
            pltpu.VMEM((2, pieces, piece_rows, depth), jnp.bfloat16),
            pltpu.SemaphoreType.DMA((2, pieces)),
        ],
    )
    return pl.pallas_call(
        merge_kernel,
        grid_spec=grid_spec,
        out_shape=[jax.ShapeDtypeStruct((pair_count, per_device, 1), jnp.float32)]
        + [jax.ShapeDtypeStruct((length, piece_rows, depth), jnp.bfloat16) for length in lengths],
        compiler_params=pltpu.CompilerParams(vmem_limit_bytes=VMEM),
        name="merge",
    )(pairs.reshape(-1), counts, where, places, rows, rows)


def place_kernel(filled_ref, quarter_ref, in_ref, *rest):
    out_ref = rest[-1]
    value = in_ref[:, 0].reshape(out_ref.shape[1], out_ref.shape[2])
    keep = pl.program_id(0) < filled_ref[0]
    out_ref[0] = jnp.where(keep, value, jnp.zeros_like(value))


def place(filled, quarter, arrived, base=None):
    sources, cap, piece_rows, depth = arrived.shape
    bases = () if base is None else (base,)
    grid_spec = pltpu.PrefetchScalarGridSpec(
        num_scalar_prefetch=2,
        grid=(cap,),
        in_specs=[pl.BlockSpec((sources, 1, piece_rows, depth), lambda s, *_: (0, s, 0, 0))]
        + [pl.BlockSpec(memory_space=pltpu.HBM)] * len(bases),
        out_specs=pl.BlockSpec(
            (1, sources * piece_rows, depth), lambda s, filled, quarter: (s, quarter[0], 0)
        ),
    )
    return pl.pallas_call(
        place_kernel,
        grid_spec=grid_spec,
        out_shape=jax.ShapeDtypeStruct((cap, QUARTERS * sources * piece_rows, depth), arrived.dtype),
        input_output_aliases={3: 0} if bases else {},
        compiler_params=pltpu.CompilerParams(vmem_limit_bytes=VMEM // 4),
        name="place",
    )(filled, quarter, arrived, *bases)


def body(gate_codes, up_codes, gate_scale, up_scale, pairs, counts, unit_order, owners):
    devices = lax.axis_size("expert")
    layers = lax.axis_size("layers")
    me = lax.axis_index("expert")
    units = gate_codes.shape[2]
    pieces = units // U
    share_units = U // devices
    size = devices // QUARTERS
    quarter = me // size
    pair_count = pairs.shape[0]
    all_pieces = pair_count * pieces

    owner_ids = owners[:, 0]
    owner_quarter = owner_ids // size
    earlier = jnp.arange(all_pieces)[None, :] < jnp.arange(all_pieces)[:, None]
    count_earlier = lambda values: jnp.sum(
        jnp.where((values[:, None] == values[None, :]) & earlier, 1, 0), axis=1
    ).astype(jnp.int32)
    slot = (owner_ids % size) * CAP + count_earlier(owner_ids)
    position = count_earlier(owner_quarter)
    where = (owner_quarter - quarter + QUARTERS) % QUARTERS
    places = jnp.where(where == 0, slot, position)
    filled = jnp.sum((owner_ids == me).astype(jnp.int32))[None]
    from_list = jnp.sum(
        jnp.where(
            (jnp.arange(size * CAP)[:, None] == slot[None, :]) & (where == 0)[None, :],
            position[None, :],
            0,
        ),
        axis=1,
    ).astype(jnp.int32)
    here = (jnp.max(position) + 1).astype(jnp.int32)
    longest = here
    for shift in range(1, layers):
        ring = [(layer, (layer + shift) % layers) for layer in range(layers)]
        longest = jnp.maximum(longest, lax.ppermute(here, "layers", ring))
    least = all_pieces // QUARTERS
    lengths = sorted({min(size * CAP, -(-least * part // 12)) for part in LIST_PARTS})
    level = sum((longest > length).astype(jnp.int32) for length in lengths[:-1])

    order = own_order(pairs, unit_order, units)
    source = order.reshape(pieces, devices, share_units).transpose(1, 0, 2).reshape(units)
    outgoing = prepare(
        source, gate_codes[0], up_codes[0], gate_scale[0], up_scale[0], devices
    )
    rows = lax.all_to_all(outgoing, "expert", split_axis=0, concat_axis=0, tiled=True)

    groups = [list(range(first, first + size)) for first in range(0, devices, size)]

    def within_quarter(value):
        value = value.reshape(size, CAP, value.shape[1], value.shape[2])
        return lax.all_to_all(
            value, "expert", split_axis=0, concat_axis=0, tiled=True, axis_index_groups=groups
        )

    def deal(listed, rows, where, places, from_list):
        similarity_part, slots, *lists = merge(
            pairs, counts, where, places, rows, size * CAP, listed
        )
        arrived = [within_quarter(slots)]
        shifts = (2, 1, 3)
        for step, shift in enumerate(shifts):
            chunk = lists[shift - 1]
            ring = [(device, (device + shift * size) % devices) for device in range(devices)]
            chunk = lax.ppermute(chunk, "expert", ring)
            spread = jnp.take(chunk, from_list, axis=0, mode="clip")
            spread, arrived[-1] = lax.optimization_barrier((spread, arrived[-1]))
            arrived.append(within_quarter(spread))
        merged, part = None, similarity_part.reshape(1, -1)
        for step, (shift, value) in enumerate(zip((0,) + shifts, arrived)):
            if step == len(shifts):
                merged, part = lax.optimization_barrier((merged, part))
            origin = ((quarter - shift + QUARTERS) % QUARTERS).astype(jnp.int32)[None]
            merged = place(filled, origin, value, merged)
        similarity = lax.all_gather(part, "expert", axis=0, tiled=True)
        similarity = similarity.reshape(devices, pair_count, pieces, share_units)
        similarity = similarity.transpose(1, 2, 0, 3).reshape(pair_count, units)
        return merged, similarity

    return lax.switch(
        level,
        [functools.partial(deal, length) for length in lengths],
        rows,
        where,
        places,
        from_list,
    )


def solution(mesh):
    in_specs = (
        P(("layers", "expert"), None, None),
        P(("layers", "expert"), None, None),
        P(("layers", "expert"), None, None),
        P(("layers", "expert"), None, None),
        P("layers", None),
        P("layers"),
        P("layers", None),
        P("layers", None),
    )
    out_specs = (P(("layers", "expert"), None, None), P("layers", None))
    return jax.shard_map(body, mesh=mesh, in_specs=in_specs, out_specs=out_specs, check_vma=False)
```

```python
import functools
import math

import jax
import jax.numpy as jnp
from jax import lax
from jax.experimental import pallas as pl
from jax.experimental.pallas import tpu as pltpu
from jax.sharding import PartitionSpec as P

BLK = 128
U = 128
LANES = 128
CAP = 6
EPSILON = 1e-06
VMEM = 60 * 1024 * 1024
QUARTERS = 4
LIST_PARTS = (14, 15, 16, 17, 18, 20, 24)


def own_order(pairs, unit_order, width):
    device_id = lax.axis_index("expert")
    is_right = pairs[:, 1] == device_id
    picked = jnp.sum(jnp.where(is_right[:, None], unit_order, 0), axis=0)
    identity = jnp.arange(width, dtype=jnp.int32)
    return jnp.where(jnp.any(is_right), picked, identity)


def prepare_kernel(source_ref, gate_ref, up_ref, gate_scale_ref, up_scale_ref, out_ref, select_ref):
    units = select_ref.shape[1]
    rows = gate_ref.shape[0]

    @pl.when(pl.program_id(0) == 0)
    def _():
        columns = lax.broadcasted_iota(jnp.int32, select_ref.shape, 1)
        select_ref[...] = (source_ref[...] == columns).astype(jnp.float32).astype(jnp.bfloat16)

    for kind, (codes_ref, scale_ref) in enumerate(
        ((gate_ref, gate_scale_ref), (up_ref, up_scale_ref))
    ):
        parts = []
        for block in range(rows // BLK):
            scale = scale_ref[0, block : block + 1, :]
            codes = codes_ref[block * BLK : (block + 1) * BLK, :].astype(jnp.float32)
            parts.append((codes * scale).astype(jnp.bfloat16))
        values = jnp.concatenate(parts, axis=0)
        chosen = lax.dot_general(
            select_ref[...], values, (((1,), (1,)), ((), ())), preferred_element_type=jnp.float32
        ).astype(jnp.bfloat16)
        out_ref[:, kind] = chosen.reshape(out_ref.shape[0], out_ref.shape[2], rows)


def prepare(source, gate_codes, up_codes, gate_scale, up_scale, devices):
    depth, units = gate_codes.shape
    per_device = units // devices
    tile = 256
    blocks = tile // BLK
    spread = lambda scale: jnp.repeat(scale.astype(jnp.float32), BLK, axis=1).reshape(
        depth // tile, blocks, units
    )
    return pl.pallas_call(
        prepare_kernel,
        grid=(depth // tile,),
        in_specs=[
            pl.BlockSpec((units, 1), lambda d: (0, 0)),
            pl.BlockSpec((tile, units), lambda d: (d, 0)),
            pl.BlockSpec((tile, units), lambda d: (d, 0)),
            pl.BlockSpec((1, blocks, units), lambda d: (d, 0, 0)),
            pl.BlockSpec((1, blocks, units), lambda d: (d, 0, 0)),
        ],
        out_specs=pl.BlockSpec((devices, 2, per_device, tile), lambda d: (0, 0, 0, d)),
        out_shape=jax.ShapeDtypeStruct((devices, 2, per_device, depth), jnp.bfloat16),
        scratch_shapes=[pltpu.VMEM((units, units), jnp.bfloat16)],
        compiler_params=pltpu.CompilerParams(vmem_limit_bytes=VMEM),
        name="prepare",
    )(source[:, None], gate_codes, up_codes, spread(gate_scale), spread(up_scale))


def merge_kernel(
    pairs_ref, counts_ref, where_ref, place_ref, left_ref, right_ref, similarity_ref, *rest
):
    outs, (woven, ready, sems) = rest[:-3], rest[-3:]
    pair = pl.program_id(0)
    pair_count = pl.num_programs(0)
    per_device, depth = left_ref.shape[2], left_ref.shape[3]
    pieces, piece_rows = ready.shape[1], ready.shape[2]
    left_gate = left_ref[0, 0].astype(jnp.float32)
    left_up = left_ref[0, 1].astype(jnp.float32)
    right_gate = right_ref[0, 0].astype(jnp.float32)
    right_up = right_ref[0, 1].astype(jnp.float32)
    total_of = lambda value: jnp.sum(value, axis=1, keepdims=True)
    intersection = total_of(left_gate * right_gate + left_up * right_up)
    left_norm = total_of(left_gate * left_gate + left_up * left_up)
    right_norm = total_of(right_gate * right_gate + right_up * right_up)
    similarity = (
        intersection
        * math.sqrt(2.0 * depth)
        / jnp.sqrt((left_norm + EPSILON) * (right_norm + EPSILON))
    )
    similarity_ref[0] = similarity
    left_freq = counts_ref[pairs_ref[2 * pair]].astype(jnp.float32)
    right_freq = counts_ref[pairs_ref[2 * pair + 1]].astype(jnp.float32)
    share = right_freq * jax.nn.sigmoid(similarity)
    total = left_freq + share
    left_weight = left_freq / total
    right_weight = share / total
    for kind, (left, right) in enumerate(((left_gate, right_gate), (left_up, right_up))):
        merged = left_weight * left + right_weight * right
        for block in range(depth // LANES):
            woven[block, pl.ds(kind, per_device, stride=2), :] = merged[
                :, block * LANES : (block + 1) * LANES
            ]
    slot = lax.rem(pair, 2)

    def each_copy(which_pair, which_slot, act):
        for piece in range(pieces):
            index = which_pair * pieces + piece
            for where, out_ref in enumerate(outs):

                @pl.when(where_ref[index] == where)
                def _():
                    act(
                        pltpu.make_async_copy(
                            ready.at[which_slot, piece],
                            out_ref.at[place_ref[index]],
                            sems.at[which_slot, piece],
                        )
                    )

    @pl.when(pair >= 2)
    def _():
        each_copy(pair - 2, slot, lambda copy: copy.wait())

    for block in range(depth // LANES):
        ready[slot, :, :, block * LANES : (block + 1) * LANES] = (
            woven[block].reshape(pieces, piece_rows, LANES).astype(jnp.bfloat16)
        )
    each_copy(pair, slot, lambda copy: copy.start())

    @pl.when(pair == pair_count - 1)
    def _():
        each_copy(pair - 1, 1 - slot, lambda copy: copy.wait())
        each_copy(pair, slot, lambda copy: copy.wait())


def merge(pairs, counts, where, places, rows, slots, listed):
    _, _, per_device, depth = rows.shape
    pair_count = pairs.shape[0]
    pieces = where.shape[0] // pair_count
    piece_rows = 2 * per_device // pieces
    lengths = (slots,) + (listed,) * (QUARTERS - 1)
    grid_spec = pltpu.PrefetchScalarGridSpec(
        num_scalar_prefetch=4,
        grid=(pair_count,),
        in_specs=[
            pl.BlockSpec((1, 2, per_device, depth), lambda p, pairs, *_: (pairs[2 * p], 0, 0, 0)),
            pl.BlockSpec(
                (1, 2, per_device, depth), lambda p, pairs, *_: (pairs[2 * p + 1], 0, 0, 0)
            ),
        ],
        out_specs=[pl.BlockSpec((1, per_device, 1), lambda p, *_: (p, 0, 0))]
        + [pl.BlockSpec(memory_space=pltpu.HBM)] * len(lengths),
        scratch_shapes=[
            pltpu.VMEM((depth // LANES, 2 * per_device, LANES), jnp.float32),
            pltpu.VMEM((2, pieces, piece_rows, depth), jnp.bfloat16),
            pltpu.SemaphoreType.DMA((2, pieces)),
        ],
    )
    return pl.pallas_call(
        merge_kernel,
        grid_spec=grid_spec,
        out_shape=[jax.ShapeDtypeStruct((pair_count, per_device, 1), jnp.float32)]
        + [jax.ShapeDtypeStruct((length, piece_rows, depth), jnp.bfloat16) for length in lengths],
        compiler_params=pltpu.CompilerParams(vmem_limit_bytes=VMEM),
        name="merge",
    )(pairs.reshape(-1), counts, where, places, rows, rows)


def place_kernel(filled_ref, quarter_ref, in_ref, *rest):
    out_ref = rest[-1]
    slots = out_ref.shape[0]
    for slot in range(slots):
        value = in_ref[:, slot].reshape(out_ref.shape[1:])
        keep = pl.program_id(0) * slots + slot < filled_ref[0]
        out_ref[slot] = jnp.where(keep, value, jnp.zeros_like(value))


def place(filled, quarter, arrived, base=None):
    sources, cap, piece_rows, depth = arrived.shape
    slots = 2
    bases = () if base is None else (base,)
    grid_spec = pltpu.PrefetchScalarGridSpec(
        num_scalar_prefetch=2,
        grid=(cap // slots,),
        in_specs=[pl.BlockSpec((sources, slots, piece_rows, depth), lambda s, *_: (0, s, 0, 0))]
        + [pl.BlockSpec(memory_space=pltpu.HBM)] * len(bases),
        out_specs=pl.BlockSpec(
            (slots, sources * piece_rows, depth), lambda s, filled, quarter: (s, quarter[0], 0)
        ),
    )
    return pl.pallas_call(
        place_kernel,
        grid_spec=grid_spec,
        out_shape=jax.ShapeDtypeStruct((cap, QUARTERS * sources * piece_rows, depth), arrived.dtype),
        input_output_aliases={3: 0} if bases else {},
        compiler_params=pltpu.CompilerParams(vmem_limit_bytes=VMEM // 4),
        name="place",
    )(filled, quarter, arrived, *bases)


def body(gate_codes, up_codes, gate_scale, up_scale, pairs, counts, unit_order, owners):
    devices = lax.axis_size("expert")
    layers = lax.axis_size("layers")
    me = lax.axis_index("expert")
    units = gate_codes.shape[2]
    pieces = units // U
    share_units = U // devices
    size = devices // QUARTERS
    quarter = me // size
    pair_count = pairs.shape[0]
    all_pieces = pair_count * pieces

    owner_ids = owners[:, 0]
    owner_quarter = owner_ids // size
    earlier = jnp.arange(all_pieces)[None, :] < jnp.arange(all_pieces)[:, None]
    count_earlier = lambda values: jnp.sum(
        jnp.where((values[:, None] == values[None, :]) & earlier, 1, 0), axis=1
    ).astype(jnp.int32)
    slot = (owner_ids % size) * CAP + count_earlier(owner_ids)
    position = count_earlier(owner_quarter)
    where = (owner_quarter - quarter + QUARTERS) % QUARTERS
    places = jnp.where(where == 0, slot, position)
    filled = jnp.sum((owner_ids == me).astype(jnp.int32))[None]
    from_list = jnp.sum(
        jnp.where(
            (jnp.arange(size * CAP)[:, None] == slot[None, :]) & (where == 0)[None, :],
            position[None, :],
            0,
        ),
        axis=1,
    ).astype(jnp.int32)
    here = (jnp.max(position) + 1).astype(jnp.int32)
    longest = here
    for shift in range(1, layers):
        ring = [(layer, (layer + shift) % layers) for layer in range(layers)]
        longest = jnp.maximum(longest, lax.ppermute(here, "layers", ring))
    least = all_pieces // QUARTERS
    lengths = sorted({min(size * CAP, -(-least * part // 12)) for part in LIST_PARTS})
    level = sum((longest > length).astype(jnp.int32) for length in lengths[:-1])

    order = own_order(pairs, unit_order, units)
    source = order.reshape(pieces, devices, share_units).transpose(1, 0, 2).reshape(units)
    outgoing = prepare(
        source, gate_codes[0], up_codes[0], gate_scale[0], up_scale[0], devices
    )
    rows = lax.all_to_all(outgoing, "expert", split_axis=0, concat_axis=0, tiled=True)

    groups = [list(range(first, first + size)) for first in range(0, devices, size)]

    def within_quarter(value):
        value = value.reshape(size, CAP, value.shape[1], value.shape[2])
        return lax.all_to_all(
            value, "expert", split_axis=0, concat_axis=0, tiled=True, axis_index_groups=groups
        )

    def deal(listed, rows, where, places, from_list):
        similarity_part, slots, *lists = merge(
            pairs, counts, where, places, rows, size * CAP, listed
        )
        arrived = [within_quarter(slots)]
        shifts = (2, 1, 3)
        for step, shift in enumerate(shifts):
            ring = [(device, (device + shift * size) % devices) for device in range(devices)]
            chunk = lax.ppermute(lists[shift - 1], "expert", ring)
            spread = jnp.take(chunk, from_list, axis=0, mode="clip")
            if step == 0:
                part, arrived[0] = lax.optimization_barrier(
                    (similarity_part.reshape(1, -1), arrived[0])
                )
                similarity = lax.all_to_all(
                    jnp.broadcast_to(part, (devices, part.shape[1])), "expert", 0, 0, tiled=True
                )
                spread, similarity = lax.optimization_barrier((spread, similarity))
            else:
                spread, arrived[-1] = lax.optimization_barrier((spread, arrived[-1]))
            arrived.append(within_quarter(spread))
        merged = None
        for shift, value in zip((0,) + shifts, arrived):
            origin = ((quarter - shift + QUARTERS) % QUARTERS).astype(jnp.int32)[None]
            merged = place(filled, origin, value, merged)
        similarity = similarity.reshape(devices, pair_count, pieces, share_units)
        similarity = similarity.transpose(1, 2, 0, 3).reshape(pair_count, units)
        return merged, similarity

    return lax.switch(
        level,
        [functools.partial(deal, length) for length in lengths],
        rows,
        where,
        places,
        from_list,
    )


def solution(mesh):
    in_specs = (
        P(("layers", "expert"), None, None),
        P(("layers", "expert"), None, None),
        P(("layers", "expert"), None, None),
        P(("layers", "expert"), None, None),
        P("layers", None),
        P("layers"),
        P("layers", None),
        P("layers", None),
    )
    out_specs = (P(("layers", "expert"), None, None), P("layers", None))
    return jax.shard_map(body, mesh=mesh, in_specs=in_specs, out_specs=out_specs, check_vma=False)
```

```python
import functools
import math

import jax
import jax.numpy as jnp
from jax import lax
from jax.experimental import pallas as pl
from jax.experimental.pallas import tpu as pltpu
from jax.sharding import PartitionSpec as P

BLK = 128
U = 128
LANES = 128
CAP = 6
EPSILON = 1e-06
VMEM = 60 * 1024 * 1024
QUARTERS = 4
LIST_PARTS = (14, 15, 16, 17, 18, 20, 24)


def prepare_kernel(
    pairs_ref, me_ref, order_ref, gate_ref, up_ref, gate_scale_ref, up_scale_ref, out_ref, select_ref, scale_ref
):
    units = select_ref.shape[1]
    tile = gate_ref.shape[0]
    devices, _, per_device, _ = out_ref.shape
    step = pl.program_id(0)

    @pl.when(step == 0)
    def _():
        order = lax.broadcasted_iota(jnp.int32, (1, units), 1)
        for pair in range(order_ref.shape[0]):
            order = jnp.where(
                pairs_ref[2 * pair + 1] == me_ref[0], order_ref[pair : pair + 1, :], order
            )
        share = U // devices
        row = lax.broadcasted_iota(jnp.int32, (units, 1), 0)
        device = lax.div(row, per_device)
        within = row - device * per_device
        piece = lax.div(within, share)
        unit = piece * U + device * share + within - piece * share
        columns = lax.broadcasted_iota(jnp.int32, (units, units), 1)
        source = jnp.sum(
            jnp.where(unit == columns, order.astype(jnp.float32), 0.0), axis=1, keepdims=True
        ).astype(jnp.int32)
        select_ref[...] = (source == columns).astype(jnp.float32).astype(jnp.bfloat16)
        for kind, scales in enumerate((gate_scale_ref, up_scale_ref)):
            value = scales[...].astype(jnp.float32)
            block = lax.div(lax.broadcasted_iota(jnp.int32, (value.shape[0], units), 1), BLK)
            spread = jnp.zeros((value.shape[0], units), jnp.float32)
            for index in range(value.shape[1]):
                spread = jnp.where(block == index, value[:, index : index + 1], spread)
            scale_ref[kind] = spread

    for kind, codes_ref in enumerate((gate_ref, up_ref)):
        parts = []
        for block in range(tile // BLK):
            scale = scale_ref[kind, pl.ds(step * (tile // BLK) + block, 1), :].astype(jnp.bfloat16)
            parts.append(codes_ref[block * BLK : (block + 1) * BLK, :] * scale)
        values = jnp.concatenate(parts, axis=0)
        chosen = lax.dot_general(
            select_ref[...], values, (((1,), (1,)), ((), ())), preferred_element_type=jnp.float32
        ).astype(jnp.bfloat16)
        out_ref[:, kind] = chosen.reshape(devices, per_device, tile)


def prepare(pairs, me, unit_order, gate_codes, up_codes, gate_scale, up_scale, devices):
    depth, units = gate_codes.shape
    per_device = units // devices
    tile = 512
    whole = lambda array: pl.BlockSpec(array.shape, lambda d, *_: (0, 0))
    grid_spec = pltpu.PrefetchScalarGridSpec(
        num_scalar_prefetch=2,
        grid=(depth // tile,),
        in_specs=[
            whole(unit_order),
            pl.BlockSpec((tile, units), lambda d, *_: (d, 0)),
            pl.BlockSpec((tile, units), lambda d, *_: (d, 0)),
            whole(gate_scale),
            whole(up_scale),
        ],
        out_specs=pl.BlockSpec((devices, 2, per_device, tile), lambda d, *_: (0, 0, 0, d)),
        scratch_shapes=[
            pltpu.VMEM((units, units), jnp.bfloat16),
            pltpu.VMEM((2, depth // BLK, units), jnp.float32),
        ],
    )
    return pl.pallas_call(
        prepare_kernel,
        grid_spec=grid_spec,
        out_shape=jax.ShapeDtypeStruct((devices, 2, per_device, depth), jnp.bfloat16),
        compiler_params=pltpu.CompilerParams(vmem_limit_bytes=VMEM),
        name="prepare",
    )(pairs.reshape(-1), me[None], unit_order, gate_codes, up_codes, gate_scale, up_scale)


def merge_kernel(
    pairs_ref, counts_ref, where_ref, place_ref, left_ref, right_ref, similarity_ref, *rest
):
    outs, (woven, ready, sems) = rest[:-3], rest[-3:]
    pair = pl.program_id(0)
    pair_count = pl.num_programs(0)
    per_device, depth = left_ref.shape[2], left_ref.shape[3]
    pieces, piece_rows = ready.shape[1], ready.shape[2]
    left_freq = counts_ref[pairs_ref[2 * pair]].astype(jnp.float32)
    right_freq = counts_ref[pairs_ref[2 * pair + 1]].astype(jnp.float32)
    group = 16 if per_device % 16 == 0 else per_device

    def values_of(first, block):
        rows, columns = slice(first, first + group), slice(block * LANES, (block + 1) * LANES)
        return [
            ref[0, kind, rows, columns].astype(jnp.float32)
            for ref in (left_ref, right_ref)
            for kind in (0, 1)
        ]

    for first in range(0, per_device, group):
        intersection = left_norm = right_norm = jnp.zeros((group, LANES), jnp.float32)
        for block in range(depth // LANES):
            left_gate, left_up, right_gate, right_up = values_of(first, block)
            intersection += left_gate * right_gate + left_up * right_up
            left_norm += left_gate * left_gate + left_up * left_up
            right_norm += right_gate * right_gate + right_up * right_up
        intersection, left_norm, right_norm = (
            jnp.sum(value, axis=1, keepdims=True) for value in (intersection, left_norm, right_norm)
        )
        similarity = (
            intersection
            * math.sqrt(2.0 * depth)
            / jnp.sqrt((left_norm + EPSILON) * (right_norm + EPSILON))
        )
        similarity_ref[0, first : first + group] = similarity
        share = right_freq * jax.nn.sigmoid(similarity)
        total = left_freq + share
        left_weight = jnp.broadcast_to(left_freq / total, (group, LANES))
        right_weight = jnp.broadcast_to(share / total, (group, LANES))
        for block in range(depth // LANES):
            left_gate, left_up, right_gate, right_up = values_of(first, block)
            woven[block, pl.ds(2 * first, group, stride=2), :] = (
                left_weight * left_gate + right_weight * right_gate
            )
            woven[block, pl.ds(2 * first + 1, group, stride=2), :] = (
                left_weight * left_up + right_weight * right_up
            )
    slot = lax.rem(pair, 2)

    def each_copy(which_pair, which_slot, act):
        for piece in range(pieces):
            index = which_pair * pieces + piece
            for where, out_ref in enumerate(outs):

                @pl.when(where_ref[index] == where)
                def _():
                    act(
                        pltpu.make_async_copy(
                            ready.at[which_slot, piece],
                            out_ref.at[place_ref[index]],
                            sems.at[which_slot, piece],
                        )
                    )

    @pl.when(pair >= 2)
    def _():
        each_copy(pair - 2, slot, lambda copy: copy.wait())

    for block in range(depth // LANES):
        ready[slot, :, :, block * LANES : (block + 1) * LANES] = (
            woven[block].reshape(pieces, piece_rows, LANES).astype(jnp.bfloat16)
        )
    each_copy(pair, slot, lambda copy: copy.start())

    @pl.when(pair == pair_count - 1)
    def _():
        each_copy(pair - 1, 1 - slot, lambda copy: copy.wait())
        each_copy(pair, slot, lambda copy: copy.wait())


def merge(pairs, counts, where, places, rows, slots, listed):
    _, _, per_device, depth = rows.shape
    pair_count = pairs.shape[0]
    pieces = where.shape[0] // pair_count
    piece_rows = 2 * per_device // pieces
    lengths = (slots,) + (listed,) * (QUARTERS - 1)
    grid_spec = pltpu.PrefetchScalarGridSpec(
        num_scalar_prefetch=4,
        grid=(pair_count,),
        in_specs=[
            pl.BlockSpec((1, 2, per_device, depth), lambda p, pairs, *_: (pairs[2 * p], 0, 0, 0)),
            pl.BlockSpec(
                (1, 2, per_device, depth), lambda p, pairs, *_: (pairs[2 * p + 1], 0, 0, 0)
            ),
        ],
        out_specs=[pl.BlockSpec((1, per_device, 1), lambda p, *_: (p, 0, 0))]
        + [pl.BlockSpec(memory_space=pltpu.HBM)] * len(lengths),
        scratch_shapes=[
            pltpu.VMEM((depth // LANES, 2 * per_device, LANES), jnp.float32),
            pltpu.VMEM((2, pieces, piece_rows, depth), jnp.bfloat16),
            pltpu.SemaphoreType.DMA((2, pieces)),
        ],
    )
    return pl.pallas_call(
        merge_kernel,
        grid_spec=grid_spec,
        out_shape=[jax.ShapeDtypeStruct((pair_count, per_device, 1), jnp.float32)]
        + [jax.ShapeDtypeStruct((length, piece_rows, depth), jnp.bfloat16) for length in lengths],
        compiler_params=pltpu.CompilerParams(vmem_limit_bytes=VMEM),
        name="merge",
    )(pairs.reshape(-1), counts, where, places, rows, rows)


def place_kernel(filled_ref, quarter_ref, in_ref, *rest):
    out_ref = rest[-1]
    slots = out_ref.shape[0]
    for slot in range(slots):
        value = in_ref[:, slot].reshape(out_ref.shape[1:])
        keep = pl.program_id(0) * slots + slot < filled_ref[0]
        out_ref[slot] = jnp.where(keep, value, jnp.zeros_like(value))


def place(filled, quarter, arrived, base=None):
    sources, cap, piece_rows, depth = arrived.shape
    slots = 2
    bases = () if base is None else (base,)
    grid_spec = pltpu.PrefetchScalarGridSpec(
        num_scalar_prefetch=2,
        grid=(cap // slots,),
        in_specs=[pl.BlockSpec((sources, slots, piece_rows, depth), lambda s, *_: (0, s, 0, 0))]
        + [pl.BlockSpec(memory_space=pltpu.HBM)] * len(bases),
        out_specs=pl.BlockSpec(
            (slots, sources * piece_rows, depth), lambda s, filled, quarter: (s, quarter[0], 0)
        ),
    )
    return pl.pallas_call(
        place_kernel,
        grid_spec=grid_spec,
        out_shape=jax.ShapeDtypeStruct((cap, QUARTERS * sources * piece_rows, depth), arrived.dtype),
        input_output_aliases={3: 0} if bases else {},
        compiler_params=pltpu.CompilerParams(vmem_limit_bytes=VMEM // 4),
        name="place",
    )(filled, quarter, arrived, *bases)


def body(gate_codes, up_codes, gate_scale, up_scale, pairs, counts, unit_order, owners):
    devices = lax.axis_size("expert")
    layers = lax.axis_size("layers")
    me = lax.axis_index("expert")
    units = gate_codes.shape[2]
    pieces = units // U
    share_units = U // devices
    size = devices // QUARTERS
    quarter = me // size
    pair_count = pairs.shape[0]
    all_pieces = pair_count * pieces

    owner_ids = owners[:, 0]
    owner_quarter = owner_ids // size
    earlier = jnp.arange(all_pieces)[None, :] < jnp.arange(all_pieces)[:, None]
    count_earlier = lambda values: jnp.sum(
        jnp.where((values[:, None] == values[None, :]) & earlier, 1, 0), axis=1
    ).astype(jnp.int32)
    slot = (owner_ids % size) * CAP + count_earlier(owner_ids)
    position = count_earlier(owner_quarter)
    where = (owner_quarter - quarter + QUARTERS) % QUARTERS
    places = jnp.where(where == 0, slot, position)
    filled = jnp.sum((owner_ids == me).astype(jnp.int32))[None]
    from_list = jnp.sum(
        jnp.where(
            (jnp.arange(size * CAP)[:, None] == slot[None, :]) & (where == 0)[None, :],
            position[None, :],
            0,
        ),
        axis=1,
    ).astype(jnp.int32)
    here = (jnp.max(position) + 1).astype(jnp.int32)
    longest = here
    for shift in range(1, layers):
        ring = [(layer, (layer + shift) % layers) for layer in range(layers)]
        longest = jnp.maximum(longest, lax.ppermute(here, "layers", ring))
    least = all_pieces // QUARTERS
    lengths = sorted({min(size * CAP, -(-least * part // 12)) for part in LIST_PARTS})
    level = sum((longest > length).astype(jnp.int32) for length in lengths[:-1])

    outgoing = prepare(
        pairs, me, unit_order, gate_codes[0], up_codes[0], gate_scale[0], up_scale[0], devices
    )
    rows = lax.all_to_all(outgoing, "expert", split_axis=0, concat_axis=0, tiled=True)

    groups = [list(range(first, first + size)) for first in range(0, devices, size)]

    def within_quarter(value):
        value = value.reshape(size, CAP, value.shape[1], value.shape[2])
        return lax.all_to_all(
            value, "expert", split_axis=0, concat_axis=0, tiled=True, axis_index_groups=groups
        )

    def deal(listed, rows, where, places, from_list):
        similarity_part, slots, *lists = merge(
            pairs, counts, where, places, rows, size * CAP, listed
        )
        arrived = [within_quarter(slots)]
        shifts = (2, 1, 3)
        for step, shift in enumerate(shifts):
            ring = [(device, (device + shift * size) % devices) for device in range(devices)]
            chunk = lax.ppermute(lists[shift - 1], "expert", ring)
            spread = jnp.take(chunk, from_list, axis=0, mode="clip")
            if step == 0:
                part, arrived[0] = lax.optimization_barrier(
                    (similarity_part.reshape(1, -1), arrived[0])
                )
                similarity = lax.all_to_all(
                    jnp.broadcast_to(part, (devices, part.shape[1])), "expert", 0, 0, tiled=True
                )
                spread, similarity = lax.optimization_barrier((spread, similarity))
            else:
                spread, arrived[-1] = lax.optimization_barrier((spread, arrived[-1]))
            arrived.append(within_quarter(spread))
        merged = None
        for shift, value in zip((0,) + shifts, arrived):
            origin = ((quarter - shift + QUARTERS) % QUARTERS).astype(jnp.int32)[None]
            merged = place(filled, origin, value, merged)
        similarity = similarity.reshape(devices, pair_count, pieces, share_units)
        similarity = similarity.transpose(1, 2, 0, 3).reshape(pair_count, units)
        return merged, similarity

    return lax.switch(
        level,
        [functools.partial(deal, length) for length in lengths],
        rows,
        where,
        places,
        from_list,
    )


def solution(mesh):
    in_specs = (
        P(("layers", "expert"), None, None),
        P(("layers", "expert"), None, None),
        P(("layers", "expert"), None, None),
        P(("layers", "expert"), None, None),
        P("layers", None),
        P("layers"),
        P("layers", None),
        P("layers", None),
    )
    out_specs = (P(("layers", "expert"), None, None), P("layers", None))
    return jax.shard_map(body, mesh=mesh, in_specs=in_specs, out_specs=out_specs, check_vma=False)
```

```python
import functools
import math

import jax
import jax.numpy as jnp
from jax import lax
from jax.experimental import pallas as pl
from jax.experimental.pallas import tpu as pltpu
from jax.sharding import PartitionSpec as P

BLK = 128
U = 128
LANES = 128
CAP = 6
EPSILON = 1e-06
VMEM = 60 * 1024 * 1024
QUARTERS = 4
LIST_PARTS = (14, 15, 16, 17, 18, 20, 24)


def prepare_kernel(
    pairs_ref, me_ref, order_ref, gate_ref, up_ref, gate_scale_ref, up_scale_ref, out_ref, select_ref, scale_ref
):
    units = select_ref.shape[1]
    tile = gate_ref.shape[0]
    devices, _, per_device, _ = out_ref.shape
    step = pl.program_id(0)

    @pl.when(step == 0)
    def _():
        order = lax.broadcasted_iota(jnp.int32, (1, units), 1)
        for pair in range(order_ref.shape[0]):
            order = jnp.where(
                pairs_ref[2 * pair + 1] == me_ref[0], order_ref[pair : pair + 1, :], order
            )
        share = U // devices
        columns = lax.broadcasted_iota(jnp.int32, (1, units), 1)
        matched = order.astype(jnp.float32)
        group = 16
        for first in range(0, units, group):
            row = first + lax.broadcasted_iota(jnp.int32, (group, 1), 0)
            device = lax.div(row, per_device)
            within = row - device * per_device
            piece = lax.div(within, share)
            unit = piece * U + device * share + within - piece * share
            source = jnp.sum(
                jnp.where(unit == columns, matched, 0.0), axis=1, keepdims=True
            ).astype(jnp.int32)
            select_ref[first : first + group] = (
                (source == columns).astype(jnp.float32).astype(jnp.bfloat16)
            )
        for kind, scales in enumerate((gate_scale_ref, up_scale_ref)):
            value = scales[...].astype(jnp.float32)
            block = lax.div(lax.broadcasted_iota(jnp.int32, (value.shape[0], units), 1), BLK)
            spread = jnp.zeros((value.shape[0], units), jnp.float32)
            for index in range(value.shape[1]):
                spread = jnp.where(block == index, value[:, index : index + 1], spread)
            scale_ref[kind] = spread

    for kind, codes_ref in enumerate((gate_ref, up_ref)):
        parts = []
        for block in range(tile // BLK):
            scale = scale_ref[kind, pl.ds(step * (tile // BLK) + block, 1), :].astype(jnp.bfloat16)
            parts.append(codes_ref[block * BLK : (block + 1) * BLK, :] * scale)
        values = jnp.concatenate(parts, axis=0)
        chosen = lax.dot_general(
            select_ref[...], values, (((1,), (1,)), ((), ())), preferred_element_type=jnp.float32
        ).astype(jnp.bfloat16)
        out_ref[:, kind] = chosen.reshape(devices, per_device, tile)


def prepare(pairs, me, unit_order, gate_codes, up_codes, gate_scale, up_scale, devices):
    depth, units = gate_codes.shape
    per_device = units // devices
    tile = 512
    whole = lambda array: pl.BlockSpec(array.shape, lambda d, *_: (0, 0))
    grid_spec = pltpu.PrefetchScalarGridSpec(
        num_scalar_prefetch=2,
        grid=(depth // tile,),
        in_specs=[
            whole(unit_order),
            pl.BlockSpec((tile, units), lambda d, *_: (d, 0)),
            pl.BlockSpec((tile, units), lambda d, *_: (d, 0)),
            whole(gate_scale),
            whole(up_scale),
        ],
        out_specs=pl.BlockSpec((devices, 2, per_device, tile), lambda d, *_: (0, 0, 0, d)),
        scratch_shapes=[
            pltpu.VMEM((units, units), jnp.bfloat16),
            pltpu.VMEM((2, depth // BLK, units), jnp.float32),
        ],
    )
    return pl.pallas_call(
        prepare_kernel,
        grid_spec=grid_spec,
        out_shape=jax.ShapeDtypeStruct((devices, 2, per_device, depth), jnp.bfloat16),
        compiler_params=pltpu.CompilerParams(vmem_limit_bytes=VMEM),
        name="prepare",
    )(pairs.reshape(-1), me[None], unit_order, gate_codes, up_codes, gate_scale, up_scale)


def merge_kernel(
    pairs_ref, counts_ref, where_ref, place_ref, rows_ref, similarity_ref, *rest
):
    outs, (held, woven, ready, arrive, sems) = rest[:-5], rest[-5:]
    pair = pl.program_id(0)
    pair_count = pl.num_programs(0)
    per_device, depth = held.shape[3], held.shape[4]
    pieces, piece_rows = ready.shape[1], ready.shape[2]

    def fetches(which_pair):
        return [
            pltpu.make_async_copy(
                rows_ref.at[pairs_ref[2 * which_pair + who], kind],
                held.at[which_pair, who, kind],
                arrive.at[which_pair, who, kind],
            )
            for who in (0, 1)
            for kind in (0, 1)
        ]

    @pl.when(pair == 0)
    def _():
        @pl.loop(0, held.shape[0])
        def _(which_pair):
            for copy in fetches(which_pair):
                copy.start()

    for copy in fetches(pair):
        copy.wait()
    left_freq = counts_ref[pairs_ref[2 * pair]].astype(jnp.float32)
    right_freq = counts_ref[pairs_ref[2 * pair + 1]].astype(jnp.float32)
    group = 16 if per_device % 16 == 0 else per_device

    def values_of(first, block):
        rows, columns = slice(first, first + group), slice(block * LANES, (block + 1) * LANES)
        return [
            held[pair, who, kind, rows, columns].astype(jnp.float32)
            for who in (0, 1)
            for kind in (0, 1)
        ]

    for first in range(0, per_device, group):
        intersection = left_norm = right_norm = jnp.zeros((group, LANES), jnp.float32)
        for block in range(depth // LANES):
            left_gate, left_up, right_gate, right_up = values_of(first, block)
            intersection += left_gate * right_gate + left_up * right_up
            left_norm += left_gate * left_gate + left_up * left_up
            right_norm += right_gate * right_gate + right_up * right_up
        intersection, left_norm, right_norm = (
            jnp.sum(value, axis=1, keepdims=True) for value in (intersection, left_norm, right_norm)
        )
        similarity = (
            intersection
            * math.sqrt(2.0 * depth)
            / jnp.sqrt((left_norm + EPSILON) * (right_norm + EPSILON))
        )
        similarity_ref[0, first : first + group] = similarity
        share = right_freq * jax.nn.sigmoid(similarity)
        total = left_freq + share
        left_weight = jnp.broadcast_to(left_freq / total, (group, LANES))
        right_weight = jnp.broadcast_to(share / total, (group, LANES))
        for block in range(depth // LANES):
            left_gate, left_up, right_gate, right_up = values_of(first, block)
            woven[block, pl.ds(2 * first, group, stride=2), :] = (
                left_weight * left_gate + right_weight * right_gate
            )
            woven[block, pl.ds(2 * first + 1, group, stride=2), :] = (
                left_weight * left_up + right_weight * right_up
            )
    slot = lax.rem(pair, 2)

    def each_copy(which_pair, which_slot, act):
        for piece in range(pieces):
            index = which_pair * pieces + piece
            for where, out_ref in enumerate(outs):

                @pl.when(where_ref[index] == where)
                def _():
                    act(
                        pltpu.make_async_copy(
                            ready.at[which_slot, piece],
                            out_ref.at[place_ref[index]],
                            sems.at[which_slot, piece],
                        )
                    )

    @pl.when(pair >= 2)
    def _():
        each_copy(pair - 2, slot, lambda copy: copy.wait())

    for block in range(depth // LANES):
        ready[slot, :, :, block * LANES : (block + 1) * LANES] = (
            woven[block].reshape(pieces, piece_rows, LANES).astype(jnp.bfloat16)
        )
    each_copy(pair, slot, lambda copy: copy.start())

    @pl.when(pair == pair_count - 1)
    def _():
        each_copy(pair - 1, 1 - slot, lambda copy: copy.wait())
        each_copy(pair, slot, lambda copy: copy.wait())


def merge(pairs, counts, where, places, rows, slots, listed):
    _, _, per_device, depth = rows.shape
    pair_count = pairs.shape[0]
    pieces = where.shape[0] // pair_count
    piece_rows = 2 * per_device // pieces
    lengths = (slots,) + (listed,) * (QUARTERS - 1)
    grid_spec = pltpu.PrefetchScalarGridSpec(
        num_scalar_prefetch=4,
        grid=(pair_count,),
        in_specs=[pl.BlockSpec(memory_space=pltpu.HBM)],
        out_specs=[pl.BlockSpec((1, per_device, 1), lambda p, *_: (p, 0, 0))]
        + [pl.BlockSpec(memory_space=pltpu.HBM)] * len(lengths),
        scratch_shapes=[
            pltpu.VMEM((pair_count, 2, 2, per_device, depth), jnp.bfloat16),
            pltpu.VMEM((depth // LANES, 2 * per_device, LANES), jnp.float32),
            pltpu.VMEM((2, pieces, piece_rows, depth), jnp.bfloat16),
            pltpu.SemaphoreType.DMA((pair_count, 2, 2)),
            pltpu.SemaphoreType.DMA((2, pieces)),
        ],
    )
    return pl.pallas_call(
        merge_kernel,
        grid_spec=grid_spec,
        out_shape=[jax.ShapeDtypeStruct((pair_count, per_device, 1), jnp.float32)]
        + [jax.ShapeDtypeStruct((length, piece_rows, depth), jnp.bfloat16) for length in lengths],
        compiler_params=pltpu.CompilerParams(vmem_limit_bytes=VMEM),
        name="merge",
    )(pairs.reshape(-1), counts, where, places, rows)


def place_kernel(filled_ref, quarter_ref, in_ref, *rest):
    out_ref = rest[-1]
    slots = out_ref.shape[0]
    for slot in range(slots):
        value = in_ref[:, slot].reshape(out_ref.shape[1:])
        keep = pl.program_id(0) * slots + slot < filled_ref[0]
        out_ref[slot] = jnp.where(keep, value, jnp.zeros_like(value))


def place(filled, quarter, arrived, base=None):
    sources, cap, piece_rows, depth = arrived.shape
    slots = 2
    bases = () if base is None else (base,)
    grid_spec = pltpu.PrefetchScalarGridSpec(
        num_scalar_prefetch=2,
        grid=(cap // slots,),
        in_specs=[pl.BlockSpec((sources, slots, piece_rows, depth), lambda s, *_: (0, s, 0, 0))]
        + [pl.BlockSpec(memory_space=pltpu.HBM)] * len(bases),
        out_specs=pl.BlockSpec(
            (slots, sources * piece_rows, depth), lambda s, filled, quarter: (s, quarter[0], 0)
        ),
    )
    return pl.pallas_call(
        place_kernel,
        grid_spec=grid_spec,
        out_shape=jax.ShapeDtypeStruct((cap, QUARTERS * sources * piece_rows, depth), arrived.dtype),
        input_output_aliases={3: 0} if bases else {},
        compiler_params=pltpu.CompilerParams(vmem_limit_bytes=VMEM // 4),
        name="place",
    )(filled, quarter, arrived, *bases)


def body(gate_codes, up_codes, gate_scale, up_scale, pairs, counts, unit_order, owners):
    devices = lax.axis_size("expert")
    layers = lax.axis_size("layers")
    me = lax.axis_index("expert")
    units = gate_codes.shape[2]
    pieces = units // U
    share_units = U // devices
    size = devices // QUARTERS
    quarter = me // size
    pair_count = pairs.shape[0]
    all_pieces = pair_count * pieces

    owner_ids = owners[:, 0]
    owner_quarter = owner_ids // size
    earlier = jnp.arange(all_pieces)[None, :] < jnp.arange(all_pieces)[:, None]
    count_earlier = lambda values: jnp.sum(
        jnp.where((values[:, None] == values[None, :]) & earlier, 1, 0), axis=1
    ).astype(jnp.int32)
    slot = (owner_ids % size) * CAP + count_earlier(owner_ids)
    position = count_earlier(owner_quarter)
    where = (owner_quarter - quarter + QUARTERS) % QUARTERS
    places = jnp.where(where == 0, slot, position)
    filled = jnp.sum((owner_ids == me).astype(jnp.int32))[None]
    from_list = jnp.sum(
        jnp.where(
            (jnp.arange(size * CAP)[:, None] == slot[None, :]) & (where == 0)[None, :],
            position[None, :],
            0,
        ),
        axis=1,
    ).astype(jnp.int32)
    here = (jnp.max(position) + 1).astype(jnp.int32)
    longest = here
    for shift in range(1, layers):
        ring = [(layer, (layer + shift) % layers) for layer in range(layers)]
        longest = jnp.maximum(longest, lax.ppermute(here, "layers", ring))
    least = all_pieces // QUARTERS
    lengths = sorted({min(size * CAP, -(-least * part // 12)) for part in LIST_PARTS})
    any_piece = longest > 0
    level = sum((longest > length).astype(jnp.int32) for length in lengths[:-1])

    outgoing = prepare(
        pairs, me, unit_order, gate_codes[0], up_codes[0], gate_scale[0], up_scale[0], devices
    )
    rows = lax.all_to_all(outgoing, "expert", split_axis=0, concat_axis=0, tiled=True)

    groups = [list(range(first, first + size)) for first in range(0, devices, size)]

    def within_quarter(value):
        value = value.reshape(size, CAP, value.shape[1], value.shape[2])
        return lax.all_to_all(
            value, "expert", split_axis=0, concat_axis=0, tiled=True, axis_index_groups=groups
        )

    def deal(listed, rows, where, places, from_list, any_piece):
        similarity_part, slots, *lists = merge(
            pairs, counts, where, places, rows, size * CAP, listed
        )
        shifts = (2, 1, 3)

        def permuted(shift, after):
            chunk, _ = lax.optimization_barrier((lists[shift - 1], after))
            ring = [(device, (device + shift * size) % devices) for device in range(devices)]
            return lax.ppermute(chunk, "expert", ring)

        def unless_empty(exchange, *values):
            shapes = jax.eval_shape(exchange, *values)
            zeros = lambda *_: jax.tree.map(lambda v: jnp.zeros(v.shape, v.dtype), shapes)
            return lax.cond(any_piece, exchange, zeros, *values)

        def spread(chunk, from_list):
            return within_quarter(jnp.take(chunk, from_list, axis=0, mode="clip"))

        def first_exchange(slots, part):
            served = within_quarter(slots)
            part, served = lax.optimization_barrier((part, served))
            spread_part = jnp.broadcast_to(part, (devices, part.shape[1]))
            return served, lax.all_to_all(spread_part, "expert", 0, 0, tiled=True)

        chunk = permuted(shifts[0], slots)
        served, similarity = unless_empty(first_exchange, slots, similarity_part.reshape(1, -1))
        arrived = [served]
        for shift in shifts[1:]:
            chunk, arrived[-1] = lax.optimization_barrier((chunk, arrived[-1]))
            following = permuted(shift, chunk)
            arrived.append(unless_empty(spread, chunk, from_list))
            chunk = following
        chunk, arrived[-1] = lax.optimization_barrier((chunk, arrived[-1]))
        arrived.append(spread(chunk, from_list))
        merged = None
        for shift, value in zip((0,) + shifts, arrived):
            origin = ((quarter - shift + QUARTERS) % QUARTERS).astype(jnp.int32)[None]
            merged = place(filled, origin, value, merged)
        similarity = similarity.reshape(devices, pair_count, pieces, share_units)
        similarity = similarity.transpose(1, 2, 0, 3).reshape(pair_count, units)
        return merged, similarity

    return lax.switch(
        level,
        [functools.partial(deal, length) for length in lengths],
        rows,
        where,
        places,
        from_list,
        any_piece,
    )


def solution(mesh):
    in_specs = (
        P(("layers", "expert"), None, None),
        P(("layers", "expert"), None, None),
        P(("layers", "expert"), None, None),
        P(("layers", "expert"), None, None),
        P("layers", None),
        P("layers"),
        P("layers", None),
        P("layers", None),
    )
    out_specs = (P(("layers", "expert"), None, None), P("layers", None))
    return jax.shard_map(body, mesh=mesh, in_specs=in_specs, out_specs=out_specs, check_vma=False)
```

```python
import functools
import math

import jax
import jax.numpy as jnp
from jax import lax
from jax.experimental import pallas as pl
from jax.experimental.pallas import tpu as pltpu
from jax.sharding import PartitionSpec as P

BLK = 128
U = 128
LANES = 128
CAP = 6
EPSILON = 1e-06
VMEM = 60 * 1024 * 1024
QUARTERS = 4
LIST_PARTS = (14, 15, 16, 17, 18, 20, 24)


def prepare_kernel(
    pairs_ref, me_ref, order_ref, gate_ref, up_ref, gate_scale_ref, up_scale_ref, out_ref, select_ref, scale_ref
):
    units = select_ref.shape[1]
    tile = gate_ref.shape[0]
    devices, _, per_device, _ = out_ref.shape
    step = pl.program_id(0)

    @pl.when(step == 0)
    def _():
        order = lax.broadcasted_iota(jnp.int32, (1, units), 1)
        for pair in range(order_ref.shape[0]):
            order = jnp.where(
                pairs_ref[1, pair] == me_ref[0], order_ref[pair : pair + 1, :], order
            )
        share = U // devices
        columns = lax.broadcasted_iota(jnp.int32, (1, units), 1)
        matched = order.astype(jnp.float32)
        group = 16
        for first in range(0, units, group):
            row = first + lax.broadcasted_iota(jnp.int32, (group, 1), 0)
            device = lax.div(row, per_device)
            within = row - device * per_device
            piece = lax.div(within, share)
            unit = piece * U + device * share + within - piece * share
            source = jnp.sum(
                jnp.where(unit == columns, matched, 0.0), axis=1, keepdims=True
            ).astype(jnp.int32)
            select_ref[first : first + group] = (
                (source == columns).astype(jnp.float32).astype(jnp.bfloat16)
            )
        for kind, scales in enumerate((gate_scale_ref, up_scale_ref)):
            blocks = scales.shape[0]
            block = lax.broadcasted_iota(jnp.int32, (blocks, units), 0)
            column = lax.broadcasted_iota(jnp.int32, (blocks, units), 1)
            covers = (lax.div(column, BLK) == block).astype(jnp.float32).astype(jnp.bfloat16)
            scale_ref[kind] = lax.dot_general(
                scales[...], covers, (((0,), (0,)), ((), ())), preferred_element_type=jnp.float32
            )

    for kind, codes_ref in enumerate((gate_ref, up_ref)):
        parts = []
        for block in range(tile // BLK):
            scale = scale_ref[kind, pl.ds(step * (tile // BLK) + block, 1), :].astype(jnp.bfloat16)
            parts.append(codes_ref[block * BLK : (block + 1) * BLK, :] * scale)
        values = jnp.concatenate(parts, axis=0)
        chosen = lax.dot_general(
            select_ref[...], values, (((1,), (1,)), ((), ())), preferred_element_type=jnp.float32
        ).astype(jnp.bfloat16)
        out_ref[:, kind] = chosen.reshape(devices, per_device, tile)


def prepare(pairs, me, unit_order, gate_codes, up_codes, gate_scale, up_scale, devices):
    depth, units = gate_codes.shape
    per_device = units // devices
    tile = 512
    whole = lambda array: pl.BlockSpec(array.shape, lambda d, *_: (0, 0))
    grid_spec = pltpu.PrefetchScalarGridSpec(
        num_scalar_prefetch=2,
        grid=(depth // tile,),
        in_specs=[
            whole(unit_order),
            pl.BlockSpec((tile, units), lambda d, *_: (d, 0)),
            pl.BlockSpec((tile, units), lambda d, *_: (d, 0)),
            whole(gate_scale),
            whole(up_scale),
        ],
        out_specs=pl.BlockSpec((devices, 2, per_device, tile), lambda d, *_: (0, 0, 0, d)),
        scratch_shapes=[
            pltpu.VMEM((units, units), jnp.bfloat16),
            pltpu.VMEM((2, depth // BLK, units), jnp.float32),
        ],
    )
    return pl.pallas_call(
        prepare_kernel,
        grid_spec=grid_spec,
        out_shape=jax.ShapeDtypeStruct((devices, 2, per_device, depth), jnp.bfloat16),
        compiler_params=pltpu.CompilerParams(vmem_limit_bytes=VMEM),
        name="prepare",
    )(pairs.T, me[None], unit_order, gate_codes, up_codes, gate_scale, up_scale)


def merge_kernel(
    pairs_ref, counts_ref, where_ref, place_ref, rows_ref, similarity_ref, *rest
):
    outs, (held, woven, ready, arrive, sems) = rest[:-5], rest[-5:]
    pair = pl.program_id(0)
    pair_count = pl.num_programs(0)
    per_device, depth = held.shape[3], held.shape[4]
    pieces, piece_rows = ready.shape[1], ready.shape[2]
    targets = (
        [(outs[0], 0)],
        [(outs[1], 0)],
        [(outs[2], 0), (outs[3], depth // 2)],
        [(outs[4], 0)],
    )

    def fetches(which_pair):
        return [
            pltpu.make_async_copy(
                rows_ref.at[pairs_ref[who, which_pair], kind],
                held.at[which_pair, who, kind],
                arrive.at[which_pair, who, kind],
            )
            for who in (0, 1)
            for kind in (0, 1)
        ]

    @pl.when(pair == 0)
    def _():
        @pl.loop(0, held.shape[0])
        def _(which_pair):
            for copy in fetches(which_pair):
                copy.start()

    for copy in fetches(pair):
        copy.wait()
    left_freq = counts_ref[pairs_ref[0, pair]].astype(jnp.float32)
    right_freq = counts_ref[pairs_ref[1, pair]].astype(jnp.float32)
    group = 16 if per_device % 16 == 0 else per_device

    def values_of(first, block):
        rows, columns = slice(first, first + group), slice(block * LANES, (block + 1) * LANES)
        return [
            held[pair, who, kind, rows, columns].astype(jnp.float32)
            for who in (0, 1)
            for kind in (0, 1)
        ]

    for first in range(0, per_device, group):
        intersection = left_norm = right_norm = jnp.zeros((group, LANES), jnp.float32)
        for block in range(depth // LANES):
            left_gate, left_up, right_gate, right_up = values_of(first, block)
            intersection += left_gate * right_gate + left_up * right_up
            left_norm += left_gate * left_gate + left_up * left_up
            right_norm += right_gate * right_gate + right_up * right_up
        intersection, left_norm, right_norm = (
            jnp.sum(value, axis=1, keepdims=True) for value in (intersection, left_norm, right_norm)
        )
        similarity = (
            intersection
            * math.sqrt(2.0 * depth)
            / jnp.sqrt((left_norm + EPSILON) * (right_norm + EPSILON))
        )
        similarity_ref[0, first : first + group] = similarity
        share = right_freq * jax.nn.sigmoid(similarity)
        total = left_freq + share
        left_weight = jnp.broadcast_to(left_freq / total, (group, LANES))
        right_weight = jnp.broadcast_to(share / total, (group, LANES))
        for block in range(depth // LANES):
            left_gate, left_up, right_gate, right_up = values_of(first, block)
            woven[block, pl.ds(2 * first, group, stride=2), :] = (
                left_weight * left_gate + right_weight * right_gate
            )
            woven[block, pl.ds(2 * first + 1, group, stride=2), :] = (
                left_weight * left_up + right_weight * right_up
            )
    slot = lax.rem(pair, 2)

    def each_copy(which_pair, which_slot, act):
        for piece in range(pieces):
            index = which_pair * pieces + piece
            for where, parts in enumerate(targets):

                @pl.when(where_ref[index] == where)
                def _():
                    for part, (out_ref, begin) in enumerate(parts):
                        act(
                            pltpu.make_async_copy(
                                ready.at[which_slot, piece, :, pl.ds(begin, out_ref.shape[-1])],
                                out_ref.at[place_ref[index]],
                                sems.at[which_slot, piece, part],
                            )
                        )

    @pl.when(pair >= 2)
    def _():
        each_copy(pair - 2, slot, lambda copy: copy.wait())

    for block in range(depth // LANES):
        ready[slot, :, :, block * LANES : (block + 1) * LANES] = (
            woven[block].reshape(pieces, piece_rows, LANES).astype(jnp.bfloat16)
        )
    each_copy(pair, slot, lambda copy: copy.start())

    @pl.when(pair == pair_count - 1)
    def _():
        each_copy(pair - 1, 1 - slot, lambda copy: copy.wait())
        each_copy(pair, slot, lambda copy: copy.wait())


def merge(pairs, counts, where, places, rows, slots, listed):
    _, _, per_device, depth = rows.shape
    pair_count = pairs.shape[0]
    pieces = where.shape[0] // pair_count
    piece_rows = 2 * per_device // pieces
    shapes = [(slots, depth), (listed, depth), (listed, depth // 2), (listed, depth // 2), (listed, depth)]
    grid_spec = pltpu.PrefetchScalarGridSpec(
        num_scalar_prefetch=4,
        grid=(pair_count,),
        in_specs=[pl.BlockSpec(memory_space=pltpu.HBM)],
        out_specs=[pl.BlockSpec((1, per_device, 1), lambda p, *_: (p, 0, 0))]
        + [pl.BlockSpec(memory_space=pltpu.HBM)] * len(shapes),
        scratch_shapes=[
            pltpu.VMEM((pair_count, 2, 2, per_device, depth), jnp.bfloat16),
            pltpu.VMEM((depth // LANES, 2 * per_device, LANES), jnp.float32),
            pltpu.VMEM((2, pieces, piece_rows, depth), jnp.bfloat16),
            pltpu.SemaphoreType.DMA((pair_count, 2, 2)),
            pltpu.SemaphoreType.DMA((2, pieces, 2)),
        ],
    )
    return pl.pallas_call(
        merge_kernel,
        grid_spec=grid_spec,
        out_shape=[jax.ShapeDtypeStruct((pair_count, per_device, 1), jnp.float32)]
        + [
            jax.ShapeDtypeStruct((length, piece_rows, width), jnp.bfloat16)
            for length, width in shapes
        ],
        compiler_params=pltpu.CompilerParams(vmem_limit_bytes=VMEM),
        name="merge",
    )(pairs.T, counts, where, places, rows)


def place_three_kernel(filled_ref, quarters_ref, *refs):
    in_refs, out_ref = refs[:-1], refs[-1]
    slots, rows, _ = out_ref.shape
    count = rows // QUARTERS
    for slot in range(slots):
        keep = pl.program_id(0) * slots + slot < filled_ref[0]
        for index, in_ref in enumerate(in_refs):
            value = in_ref[:, slot].reshape(count, out_ref.shape[2])
            first = pl.multiple_of(quarters_ref[index] * count, count)
            out_ref[slot, pl.ds(first, count), :] = jnp.where(keep, value, jnp.zeros_like(value))


def place_three(filled, quarters, arrived):
    sources, cap, piece_rows, depth = arrived[0].shape
    slots = 2
    rows = QUARTERS * sources * piece_rows
    grid_spec = pltpu.PrefetchScalarGridSpec(
        num_scalar_prefetch=2,
        grid=(cap // slots,),
        in_specs=[pl.BlockSpec((sources, slots, piece_rows, depth), lambda s, *_: (0, s, 0, 0))]
        * len(arrived),
        out_specs=pl.BlockSpec((slots, rows, depth), lambda s, *_: (s, 0, 0)),
    )
    return pl.pallas_call(
        place_three_kernel,
        grid_spec=grid_spec,
        out_shape=jax.ShapeDtypeStruct((cap, rows, depth), arrived[0].dtype),
        compiler_params=pltpu.CompilerParams(vmem_limit_bytes=VMEM // 2),
        name="place_three",
    )(filled, quarters, *arrived)


def place_kernel(filled_ref, quarter_ref, in_ref, base_ref, out_ref):
    slots = out_ref.shape[0]
    for slot in range(slots):
        value = in_ref[:, slot].reshape(out_ref.shape[1:])
        keep = pl.program_id(0) * slots + slot < filled_ref[0]
        out_ref[slot] = jnp.where(keep, value, jnp.zeros_like(value))


def place(filled, quarter, arrived, part, base):
    sources, cap, piece_rows, width = arrived.shape
    slots = 2
    grid_spec = pltpu.PrefetchScalarGridSpec(
        num_scalar_prefetch=2,
        grid=(cap // slots,),
        in_specs=[
            pl.BlockSpec((sources, slots, piece_rows, width), lambda s, *_: (0, s, 0, 0)),
            pl.BlockSpec(memory_space=pltpu.HBM),
        ],
        out_specs=pl.BlockSpec(
            (slots, sources * piece_rows, width), lambda s, filled, quarter: (s, quarter[0], part)
        ),
    )
    return pl.pallas_call(
        place_kernel,
        grid_spec=grid_spec,
        out_shape=jax.ShapeDtypeStruct(base.shape, base.dtype),
        input_output_aliases={3: 0},
        compiler_params=pltpu.CompilerParams(vmem_limit_bytes=VMEM // 4),
        name="place",
    )(filled, quarter, arrived, base)


def body(gate_codes, up_codes, gate_scale, up_scale, pairs, counts, unit_order, owners):
    devices = lax.axis_size("expert")
    layers = lax.axis_size("layers")
    me = lax.axis_index("expert")
    units = gate_codes.shape[2]
    pieces = units // U
    share_units = U // devices
    size = devices // QUARTERS
    quarter = me // size
    pair_count = pairs.shape[0]
    all_pieces = pair_count * pieces

    owner_ids = owners[:, 0]
    owner_quarter = owner_ids // size
    earlier = jnp.arange(all_pieces)[None, :] < jnp.arange(all_pieces)[:, None]
    count_earlier = lambda values: jnp.sum(
        jnp.where((values[:, None] == values[None, :]) & earlier, 1, 0), axis=1
    ).astype(jnp.int32)
    slot = (owner_ids % size) * CAP + count_earlier(owner_ids)
    position = count_earlier(owner_quarter)
    where = (owner_quarter - quarter + QUARTERS) % QUARTERS
    places = jnp.where(where == 0, slot, position)
    filled = jnp.sum((owner_ids == me).astype(jnp.int32))[None]
    from_list = jnp.sum(
        jnp.where(
            (jnp.arange(size * CAP)[:, None] == slot[None, :]) & (where == 0)[None, :],
            position[None, :],
            0,
        ),
        axis=1,
    ).astype(jnp.int32)
    here = (jnp.max(position) + 1).astype(jnp.int32)
    longest = here
    for shift in range(1, layers):
        ring = [(layer, (layer + shift) % layers) for layer in range(layers)]
        longest = jnp.maximum(longest, lax.ppermute(here, "layers", ring))
    least = all_pieces // QUARTERS
    lengths = sorted({min(size * CAP, -(-least * part // 12)) for part in LIST_PARTS})
    any_piece = longest > 0
    level = sum((longest > length).astype(jnp.int32) for length in lengths[:-1])

    outgoing = prepare(
        pairs, me, unit_order, gate_codes[0], up_codes[0], gate_scale[0].T, up_scale[0].T, devices
    )
    rows = lax.all_to_all(outgoing, "expert", split_axis=0, concat_axis=0, tiled=True)

    groups = [list(range(first, first + size)) for first in range(0, devices, size)]

    def within_quarter(value):
        value = value.reshape(size, CAP, value.shape[1], value.shape[2])
        return lax.all_to_all(
            value, "expert", split_axis=0, concat_axis=0, tiled=True, axis_index_groups=groups
        )

    def deal(listed, rows, where, places, from_list, any_piece):
        similarity_part, slots, next_list, far_first, far_second, last_list = merge(
            pairs, counts, where, places, rows, size * CAP, listed
        )
        origins = jnp.stack([(quarter - shift + QUARTERS) % QUARTERS for shift in range(QUARTERS)])
        origins = origins.astype(jnp.int32)

        def permuted(chunk, shift):
            ring = [(device, (device + shift * size) % devices) for device in range(devices)]
            return lax.ppermute(chunk, "expert", ring)

        def in_order(*values):
            return lax.optimization_barrier(values)

        def unless_empty(exchange, *values):
            shapes = jax.eval_shape(exchange, *values)
            zeros = lambda *_: jax.tree.map(lambda v: jnp.zeros(v.shape, v.dtype), shapes)
            return lax.cond(any_piece, exchange, zeros, *values)

        def spread(chunk, from_list):
            return within_quarter(jnp.take(chunk, from_list, axis=0, mode="clip"))

        def spread_and_place(chunk, from_list, filled, quarters, *arrived):
            return spread(chunk, from_list), place_three(filled, quarters, arrived)

        one_on = permuted(next_list, 1)
        own = unless_empty(within_quarter, slots)
        one_on, own = in_order(one_on, own)
        last_list, _ = in_order(last_list, one_on)
        three_on = permuted(last_list, 3)
        from_one = unless_empty(spread, one_on, from_list)
        three_on, from_one = in_order(three_on, from_one)
        far_first, _ = in_order(far_first, three_on)
        two_on = permuted(far_first, 2)
        from_three = unless_empty(spread, three_on, from_list)
        two_on, from_three = in_order(two_on, from_three)
        far_second, _ = in_order(far_second, two_on)
        rest_on = permuted(far_second, 2)
        from_two, merged = unless_empty(
            spread_and_place,
            two_on,
            from_list,
            filled,
            origins[jnp.array([0, 1, 3])],
            own,
            from_one,
            from_three,
        )
        part, from_two = in_order(similarity_part.reshape(1, -1), from_two)
        similarity = lax.all_to_all(
            jnp.broadcast_to(part, (devices, part.shape[1])), "expert", 0, 0, tiled=True
        )
        rest_on, similarity = in_order(rest_on, similarity)
        from_rest = spread(rest_on, from_list)
        merged = place(filled, origins[2:3], from_two, 0, merged)
        merged = place(filled, origins[2:3], from_rest, 1, merged)
        similarity = similarity.reshape(devices, pair_count, pieces, share_units)
        similarity = similarity.transpose(1, 2, 0, 3).reshape(pair_count, units)
        return merged, similarity

    return lax.switch(
        level,
        [functools.partial(deal, length) for length in lengths],
        rows,
        where,
        places,
        from_list,
        any_piece,
    )


def solution(mesh):
    in_specs = (
        P(("layers", "expert"), None, None),
        P(("layers", "expert"), None, None),
        P(("layers", "expert"), None, None),
        P(("layers", "expert"), None, None),
        P("layers", None),
        P("layers"),
        P("layers", None),
        P("layers", None),
    )
    out_specs = (P(("layers", "expert"), None, None), P("layers", None))
    return jax.shard_map(body, mesh=mesh, in_specs=in_specs, out_specs=out_specs, check_vma=False)
```

```python
import functools
import math

import jax
import jax.numpy as jnp
from jax import lax
from jax.experimental import pallas as pl
from jax.experimental.pallas import tpu as pltpu
from jax.sharding import PartitionSpec as P

BLK = 128
U = 128
LANES = 128
CAP = 6
EPSILON = 1e-06
VMEM = 60 * 1024 * 1024
QUARTERS = 4
LIST_PARTS = (14, 15, 16, 17, 18, 20, 24)


def prepare_kernel(
    pairs_ref, me_ref, order_ref, gate_ref, up_ref, gate_scale_ref, up_scale_ref, out_ref, select_ref, scale_ref
):
    units = select_ref.shape[1]
    tile = gate_ref.shape[0]
    devices, _, per_device, _ = out_ref.shape
    step = pl.program_id(0)

    @pl.when(step == 0)
    def _():
        order = lax.broadcasted_iota(jnp.int32, (1, units), 1)
        for pair in range(order_ref.shape[0]):
            order = jnp.where(
                pairs_ref[1, pair] == me_ref[0], order_ref[pair : pair + 1, :], order
            )
        share = U // devices
        columns = lax.broadcasted_iota(jnp.int32, (1, units), 1)
        matched = order.astype(jnp.float32)
        group = 16
        for first in range(0, units, group):
            row = first + lax.broadcasted_iota(jnp.int32, (group, 1), 0)
            device = lax.div(row, per_device)
            within = row - device * per_device
            piece = lax.div(within, share)
            unit = piece * U + device * share + within - piece * share
            source = jnp.sum(
                jnp.where(unit == columns, matched, 0.0), axis=1, keepdims=True
            ).astype(jnp.int32)
            select_ref[first : first + group] = (
                (source == columns).astype(jnp.float32).astype(jnp.bfloat16)
            )
        for kind, scales in enumerate((gate_scale_ref, up_scale_ref)):
            blocks = scales.shape[0]
            block = lax.broadcasted_iota(jnp.int32, (blocks, units), 0)
            column = lax.broadcasted_iota(jnp.int32, (blocks, units), 1)
            covers = (lax.div(column, BLK) == block).astype(jnp.float32).astype(jnp.bfloat16)
            scale_ref[kind] = lax.dot_general(
                scales[...], covers, (((0,), (0,)), ((), ())), preferred_element_type=jnp.float32
            )

    for kind, codes_ref in enumerate((gate_ref, up_ref)):
        parts = []
        for block in range(tile // BLK):
            scale = scale_ref[kind, pl.ds(step * (tile // BLK) + block, 1), :].astype(jnp.bfloat16)
            parts.append(codes_ref[block * BLK : (block + 1) * BLK, :] * scale)
        values = jnp.concatenate(parts, axis=0)
        chosen = lax.dot_general(
            select_ref[...], values, (((1,), (1,)), ((), ())), preferred_element_type=jnp.float32
        ).astype(jnp.bfloat16)
        out_ref[:, kind] = chosen.reshape(devices, per_device, tile)


def prepare(pairs, me, unit_order, gate_codes, up_codes, gate_scale, up_scale, devices):
    depth, units = gate_codes.shape
    per_device = units // devices
    tile = 512
    whole = lambda array: pl.BlockSpec(array.shape, lambda d, *_: (0, 0))
    grid_spec = pltpu.PrefetchScalarGridSpec(
        num_scalar_prefetch=2,
        grid=(depth // tile,),
        in_specs=[
            whole(unit_order),
            pl.BlockSpec((tile, units), lambda d, *_: (d, 0)),
            pl.BlockSpec((tile, units), lambda d, *_: (d, 0)),
            whole(gate_scale),
            whole(up_scale),
        ],
        out_specs=pl.BlockSpec((devices, 2, per_device, tile), lambda d, *_: (0, 0, 0, d)),
        scratch_shapes=[
            pltpu.VMEM((units, units), jnp.bfloat16),
            pltpu.VMEM((2, depth // BLK, units), jnp.float32),
        ],
    )
    return pl.pallas_call(
        prepare_kernel,
        grid_spec=grid_spec,
        out_shape=jax.ShapeDtypeStruct((devices, 2, per_device, depth), jnp.bfloat16),
        compiler_params=pltpu.CompilerParams(vmem_limit_bytes=VMEM),
        name="prepare",
    )(pairs.T, me[None], unit_order, gate_codes, up_codes, gate_scale, up_scale)


def merge_kernel(
    pairs_ref, counts_ref, where_ref, place_ref, rows_ref, similarity_ref, *rest
):
    outs, (held, woven, ready, arrive, sems) = rest[:-5], rest[-5:]
    pair = pl.program_id(0)
    pair_count = pl.num_programs(0)
    per_device, depth = held.shape[3], held.shape[4]
    pieces, piece_rows = ready.shape[1], ready.shape[2]
    targets = (
        [(outs[0], 0)],
        [(outs[1], 0)],
        [(outs[2], 0), (outs[3], depth // 2)],
        [(outs[4], 0)],
    )

    def fetches(which_pair):
        return [
            pltpu.make_async_copy(
                rows_ref.at[pairs_ref[who, which_pair], kind],
                held.at[which_pair, who, kind],
                arrive.at[which_pair, who, kind],
            )
            for who in (0, 1)
            for kind in (0, 1)
        ]

    @pl.when(pair == 0)
    def _():
        @pl.loop(0, held.shape[0])
        def _(which_pair):
            for copy in fetches(which_pair):
                copy.start()

    for copy in fetches(pair):
        copy.wait()
    left_freq = counts_ref[pairs_ref[0, pair]].astype(jnp.float32)
    right_freq = counts_ref[pairs_ref[1, pair]].astype(jnp.float32)
    group = 16 if per_device % 16 == 0 else per_device

    def values_of(first, block):
        rows, columns = slice(first, first + group), slice(block * LANES, (block + 1) * LANES)
        return [
            held[pair, who, kind, rows, columns].astype(jnp.float32)
            for who in (0, 1)
            for kind in (0, 1)
        ]

    for first in range(0, per_device, group):
        intersection = left_norm = right_norm = jnp.zeros((group, LANES), jnp.float32)
        for block in range(depth // LANES):
            left_gate, left_up, right_gate, right_up = values_of(first, block)
            intersection += left_gate * right_gate + left_up * right_up
            left_norm += left_gate * left_gate + left_up * left_up
            right_norm += right_gate * right_gate + right_up * right_up
        intersection, left_norm, right_norm = (
            jnp.sum(value, axis=1, keepdims=True) for value in (intersection, left_norm, right_norm)
        )
        similarity = (
            intersection
            * math.sqrt(2.0 * depth)
            / jnp.sqrt((left_norm + EPSILON) * (right_norm + EPSILON))
        )
        similarity_ref[0, first : first + group] = similarity
        share = right_freq * jax.nn.sigmoid(similarity)
        total = left_freq + share
        left_weight = jnp.broadcast_to(left_freq / total, (group, LANES))
        right_weight = jnp.broadcast_to(share / total, (group, LANES))
        for block in range(depth // LANES):
            left_gate, left_up, right_gate, right_up = values_of(first, block)
            woven[block, pl.ds(2 * first, group, stride=2), :] = (
                left_weight * left_gate + right_weight * right_gate
            )
            woven[block, pl.ds(2 * first + 1, group, stride=2), :] = (
                left_weight * left_up + right_weight * right_up
            )
    def each_copy(which_pair, act):
        for piece in range(pieces):
            index = which_pair * pieces + piece
            for where, parts in enumerate(targets):

                @pl.when(where_ref[index] == where)
                def _():
                    for part, (out_ref, begin) in enumerate(parts):
                        act(
                            pltpu.make_async_copy(
                                ready.at[which_pair, piece, :, pl.ds(begin, out_ref.shape[-1])],
                                out_ref.at[place_ref[index]],
                                sems.at[which_pair, piece, part],
                            )
                        )

    for block in range(depth // LANES):
        ready[pair, :, :, block * LANES : (block + 1) * LANES] = (
            woven[block].reshape(pieces, piece_rows, LANES).astype(jnp.bfloat16)
        )
    each_copy(pair, lambda copy: copy.start())

    @pl.when(pair == pair_count - 1)
    def _():
        @pl.loop(0, ready.shape[0])
        def _(which_pair):
            each_copy(which_pair, lambda copy: copy.wait())


def merge(pairs, counts, where, places, rows, slots, listed):
    _, _, per_device, depth = rows.shape
    pair_count = pairs.shape[0]
    pieces = where.shape[0] // pair_count
    piece_rows = 2 * per_device // pieces
    shapes = [(slots, depth), (listed, depth), (listed, depth // 2), (listed, depth // 2), (listed, depth)]
    grid_spec = pltpu.PrefetchScalarGridSpec(
        num_scalar_prefetch=4,
        grid=(pair_count,),
        in_specs=[pl.BlockSpec(memory_space=pltpu.HBM)],
        out_specs=[pl.BlockSpec((1, per_device, 1), lambda p, *_: (p, 0, 0))]
        + [pl.BlockSpec(memory_space=pltpu.HBM)] * len(shapes),
        scratch_shapes=[
            pltpu.VMEM((pair_count, 2, 2, per_device, depth), jnp.bfloat16),
            pltpu.VMEM((depth // LANES, 2 * per_device, LANES), jnp.float32),
            pltpu.VMEM((pair_count, pieces, piece_rows, depth), jnp.bfloat16),
            pltpu.SemaphoreType.DMA((pair_count, 2, 2)),
            pltpu.SemaphoreType.DMA((pair_count, pieces, 2)),
        ],
    )
    return pl.pallas_call(
        merge_kernel,
        grid_spec=grid_spec,
        out_shape=[jax.ShapeDtypeStruct((pair_count, per_device, 1), jnp.float32)]
        + [
            jax.ShapeDtypeStruct((length, piece_rows, width), jnp.bfloat16)
            for length, width in shapes
        ],
        compiler_params=pltpu.CompilerParams(vmem_limit_bytes=VMEM),
        name="merge",
    )(pairs.T, counts, where, places, rows)


def place_three_kernel(filled_ref, quarters_ref, *refs):
    in_refs, out_ref = refs[:-1], refs[-1]
    slots, rows, _ = out_ref.shape
    count = rows // QUARTERS
    for slot in range(slots):
        keep = pl.program_id(0) * slots + slot < filled_ref[0]
        for index, in_ref in enumerate(in_refs):
            value = in_ref[:, slot].reshape(count, out_ref.shape[2])
            first = pl.multiple_of(quarters_ref[index] * count, count)
            out_ref[slot, pl.ds(first, count), :] = jnp.where(keep, value, jnp.zeros_like(value))


def place_three(filled, quarters, arrived):
    sources, cap, piece_rows, depth = arrived[0].shape
    slots = 2
    rows = QUARTERS * sources * piece_rows
    grid_spec = pltpu.PrefetchScalarGridSpec(
        num_scalar_prefetch=2,
        grid=(cap // slots,),
        in_specs=[pl.BlockSpec((sources, slots, piece_rows, depth), lambda s, *_: (0, s, 0, 0))]
        * len(arrived),
        out_specs=pl.BlockSpec((slots, rows, depth), lambda s, *_: (s, 0, 0)),
    )
    return pl.pallas_call(
        place_three_kernel,
        grid_spec=grid_spec,
        out_shape=jax.ShapeDtypeStruct((cap, rows, depth), arrived[0].dtype),
        compiler_params=pltpu.CompilerParams(vmem_limit_bytes=VMEM // 2),
        name="place_three",
    )(filled, quarters, *arrived)


def place_kernel(filled_ref, quarter_ref, in_ref, base_ref, out_ref):
    slots = out_ref.shape[0]
    for slot in range(slots):
        value = in_ref[:, slot].reshape(out_ref.shape[1:])
        keep = pl.program_id(0) * slots + slot < filled_ref[0]
        out_ref[slot] = jnp.where(keep, value, jnp.zeros_like(value))


def place(filled, quarter, arrived, part, base):
    sources, cap, piece_rows, width = arrived.shape
    slots = 2
    grid_spec = pltpu.PrefetchScalarGridSpec(
        num_scalar_prefetch=2,
        grid=(cap // slots,),
        in_specs=[
            pl.BlockSpec((sources, slots, piece_rows, width), lambda s, *_: (0, s, 0, 0)),
            pl.BlockSpec(memory_space=pltpu.HBM),
        ],
        out_specs=pl.BlockSpec(
            (slots, sources * piece_rows, width), lambda s, filled, quarter: (s, quarter[0], part)
        ),
    )
    return pl.pallas_call(
        place_kernel,
        grid_spec=grid_spec,
        out_shape=jax.ShapeDtypeStruct(base.shape, base.dtype),
        input_output_aliases={3: 0},
        compiler_params=pltpu.CompilerParams(vmem_limit_bytes=VMEM // 4),
        name="place",
    )(filled, quarter, arrived, base)


def body(gate_codes, up_codes, gate_scale, up_scale, pairs, counts, unit_order, owners):
    devices = lax.axis_size("expert")
    layers = lax.axis_size("layers")
    me = lax.axis_index("expert")
    units = gate_codes.shape[2]
    pieces = units // U
    share_units = U // devices
    size = devices // QUARTERS
    quarter = me // size
    pair_count = pairs.shape[0]
    all_pieces = pair_count * pieces

    owner_ids = owners[:, 0]
    owner_quarter = owner_ids // size
    earlier = jnp.arange(all_pieces)[None, :] < jnp.arange(all_pieces)[:, None]
    count_earlier = lambda values: jnp.sum(
        jnp.where((values[:, None] == values[None, :]) & earlier, 1, 0), axis=1
    ).astype(jnp.int32)
    slot = (owner_ids % size) * CAP + count_earlier(owner_ids)
    position = count_earlier(owner_quarter)
    where = (owner_quarter - quarter + QUARTERS) % QUARTERS
    places = jnp.where(where == 0, slot, position)
    filled = jnp.sum((owner_ids == me).astype(jnp.int32))[None]
    from_list = jnp.sum(
        jnp.where(
            (jnp.arange(size * CAP)[:, None] == slot[None, :]) & (where == 0)[None, :],
            position[None, :],
            0,
        ),
        axis=1,
    ).astype(jnp.int32)
    here = (jnp.max(position) + 1).astype(jnp.int32)
    longest = here
    for shift in range(1, layers):
        ring = [(layer, (layer + shift) % layers) for layer in range(layers)]
        longest = jnp.maximum(longest, lax.ppermute(here, "layers", ring))
    least = all_pieces // QUARTERS
    lengths = sorted({min(size * CAP, -(-least * part // 12)) for part in LIST_PARTS})
    any_piece = longest > 0
    level = sum((longest > length).astype(jnp.int32) for length in lengths[:-1])

    outgoing = prepare(
        pairs, me, unit_order, gate_codes[0], up_codes[0], gate_scale[0].T, up_scale[0].T, devices
    )
    rows = lax.all_to_all(outgoing, "expert", split_axis=0, concat_axis=0, tiled=True)

    groups = [list(range(first, first + size)) for first in range(0, devices, size)]

    def within_quarter(value):
        value = value.reshape(size, CAP, value.shape[1], value.shape[2])
        return lax.all_to_all(
            value, "expert", split_axis=0, concat_axis=0, tiled=True, axis_index_groups=groups
        )

    def deal(listed, rows, where, places, from_list, any_piece):
        similarity_part, slots, next_list, far_first, far_second, last_list = merge(
            pairs, counts, where, places, rows, size * CAP, listed
        )
        origins = jnp.stack([(quarter - shift + QUARTERS) % QUARTERS for shift in range(QUARTERS)])
        origins = origins.astype(jnp.int32)

        def permuted(chunk, shift):
            ring = [(device, (device + shift * size) % devices) for device in range(devices)]
            return lax.ppermute(chunk, "expert", ring)

        def in_order(*values):
            return lax.optimization_barrier(values)

        def unless_empty(exchange, *values):
            shapes = jax.eval_shape(exchange, *values)
            zeros = lambda *_: jax.tree.map(lambda v: jnp.zeros(v.shape, v.dtype), shapes)
            return lax.cond(any_piece, exchange, zeros, *values)

        def spread(chunk, from_list):
            return within_quarter(jnp.take(chunk, from_list, axis=0, mode="clip"))

        def spread_and_place(chunk, from_list, filled, quarters, *arrived):
            return spread(chunk, from_list), place_three(filled, quarters, arrived)

        def spread_and_place_part(chunk, from_list, filled, quarter, arrived, merged):
            return spread(chunk, from_list), place(filled, quarter, arrived, 0, merged)

        similarity = lax.all_to_all(
            jnp.broadcast_to(similarity_part.reshape(1, -1), (devices, similarity_part.size)),
            "expert",
            0,
            0,
            tiled=True,
        )
        next_list, slots, similarity = in_order(next_list, slots, similarity)
        one_on = permuted(next_list, 1)
        own = unless_empty(within_quarter, slots)
        one_on, own = in_order(one_on, own)
        last_list, _ = in_order(last_list, one_on)
        three_on = permuted(last_list, 3)
        from_one = unless_empty(spread, one_on, from_list)
        three_on, from_one = in_order(three_on, from_one)
        far_first, _ = in_order(far_first, three_on)
        two_on = permuted(far_first, 2)
        from_three = unless_empty(spread, three_on, from_list)
        two_on, from_three = in_order(two_on, from_three)
        far_second, _ = in_order(far_second, two_on)
        rest_on = permuted(far_second, 2)
        from_two, merged = unless_empty(
            spread_and_place,
            two_on,
            from_list,
            filled,
            origins[jnp.array([0, 1, 3])],
            own,
            from_one,
            from_three,
        )
        from_rest, merged = unless_empty(
            spread_and_place_part, rest_on, from_list, filled, origins[2:3], from_two, merged
        )
        merged = place(filled, origins[2:3], from_rest, 1, merged)
        similarity = similarity.reshape(devices, pair_count, pieces, share_units)
        similarity = similarity.transpose(1, 2, 0, 3).reshape(pair_count, units)
        return merged, similarity

    return lax.switch(
        level,
        [functools.partial(deal, length) for length in lengths],
        rows,
        where,
        places,
        from_list,
        any_piece,
    )


def solution(mesh):
    in_specs = (
        P(("layers", "expert"), None, None),
        P(("layers", "expert"), None, None),
        P(("layers", "expert"), None, None),
        P(("layers", "expert"), None, None),
        P("layers", None),
        P("layers"),
        P("layers", None),
        P("layers", None),
    )
    out_specs = (P(("layers", "expert"), None, None), P("layers", None))
    return jax.shard_map(body, mesh=mesh, in_specs=in_specs, out_specs=out_specs, check_vma=False)
```

```python
import functools
import math

import jax
import jax.numpy as jnp
from jax import lax
from jax.experimental import pallas as pl
from jax.experimental.pallas import tpu as pltpu
from jax.sharding import PartitionSpec as P

BLK = 128
U = 128
LANES = 128
CAP = 6
EPSILON = 1e-06
VMEM = 60 * 1024 * 1024
QUARTERS = 4
LIST_PARTS = (15, 16, 17, 18, 19, 20, 24)


def prepare_kernel(
    pairs_ref, me_ref, order_ref, gate_ref, up_ref, gate_scale_ref, up_scale_ref, out_ref, select_ref, scale_ref
):
    units = select_ref.shape[1]
    tile = gate_ref.shape[0]
    devices, _, per_device, _ = out_ref.shape
    step = pl.program_id(0)

    @pl.when(step == 0)
    def _():
        order = lax.broadcasted_iota(jnp.int32, (1, units), 1)
        for pair in range(order_ref.shape[0]):
            order = jnp.where(
                pairs_ref[1, pair] == me_ref[0], order_ref[pair : pair + 1, :], order
            )
        share = U // devices
        columns = lax.broadcasted_iota(jnp.int32, (1, units), 1)
        matched = order.astype(jnp.float32)
        group = 16
        for first in range(0, units, group):
            row = first + lax.broadcasted_iota(jnp.int32, (group, 1), 0)
            device = lax.div(row, per_device)
            within = row - device * per_device
            piece = lax.div(within, share)
            unit = piece * U + device * share + within - piece * share
            source = jnp.sum(
                jnp.where(unit == columns, matched, 0.0), axis=1, keepdims=True
            ).astype(jnp.int32)
            select_ref[first : first + group] = (
                (source == columns).astype(jnp.float32).astype(jnp.bfloat16)
            )
        for kind, scales in enumerate((gate_scale_ref, up_scale_ref)):
            blocks = scales.shape[0]
            block = lax.broadcasted_iota(jnp.int32, (blocks, units), 0)
            column = lax.broadcasted_iota(jnp.int32, (blocks, units), 1)
            covers = (lax.div(column, BLK) == block).astype(jnp.float32).astype(jnp.bfloat16)
            scale_ref[kind] = lax.dot_general(
                scales[...], covers, (((0,), (0,)), ((), ())), preferred_element_type=jnp.float32
            )

    for kind, codes_ref in enumerate((gate_ref, up_ref)):
        parts = []
        for block in range(tile // BLK):
            scale = scale_ref[kind, pl.ds(step * (tile // BLK) + block, 1), :].astype(jnp.bfloat16)
            parts.append(codes_ref[block * BLK : (block + 1) * BLK, :] * scale)
        values = jnp.concatenate(parts, axis=0)
        chosen = lax.dot_general(
            select_ref[...], values, (((1,), (1,)), ((), ())), preferred_element_type=jnp.float32
        ).astype(jnp.bfloat16)
        out_ref[:, kind] = chosen.reshape(devices, per_device, tile)


def prepare(pairs, me, unit_order, gate_codes, up_codes, gate_scale, up_scale, devices):
    depth, units = gate_codes.shape
    per_device = units // devices
    tile = 512
    whole = lambda array: pl.BlockSpec(array.shape, lambda d, *_: (0, 0))
    grid_spec = pltpu.PrefetchScalarGridSpec(
        num_scalar_prefetch=2,
        grid=(depth // tile,),
        in_specs=[
            whole(unit_order),
            pl.BlockSpec((tile, units), lambda d, *_: (d, 0)),
            pl.BlockSpec((tile, units), lambda d, *_: (d, 0)),
            whole(gate_scale),
            whole(up_scale),
        ],
        out_specs=pl.BlockSpec((devices, 2, per_device, tile), lambda d, *_: (0, 0, 0, d)),
        scratch_shapes=[
            pltpu.VMEM((units, units), jnp.bfloat16),
            pltpu.VMEM((2, depth // BLK, units), jnp.float32),
        ],
    )
    return pl.pallas_call(
        prepare_kernel,
        grid_spec=grid_spec,
        out_shape=jax.ShapeDtypeStruct((devices, 2, per_device, depth), jnp.bfloat16),
        compiler_params=pltpu.CompilerParams(vmem_limit_bytes=VMEM),
        name="prepare",
    )(pairs.T, me[None], unit_order, gate_codes, up_codes, gate_scale, up_scale)


def merge_kernel(
    pairs_ref, counts_ref, where_ref, place_ref, rows_ref, similarity_ref, *rest
):
    outs, (held, woven, ready, arrive, sems) = rest[:-5], rest[-5:]
    pair = pl.program_id(0)
    pair_count = pl.num_programs(0)
    per_device, depth = held.shape[3], held.shape[4]
    pieces, piece_rows = ready.shape[1], ready.shape[2]
    targets = (
        [(outs[0], 0)],
        [(outs[1], 0)],
        [(outs[2], 0), (outs[3], depth // 2)],
        [(outs[4], 0)],
    )

    def fetches(which_pair):
        return [
            pltpu.make_async_copy(
                rows_ref.at[pairs_ref[who, which_pair], kind],
                held.at[which_pair, who, kind],
                arrive.at[which_pair, who, kind],
            )
            for who in (0, 1)
            for kind in (0, 1)
        ]

    @pl.when(pair == 0)
    def _():
        @pl.loop(0, held.shape[0])
        def _(which_pair):
            for copy in fetches(which_pair):
                copy.start()

    for copy in fetches(pair):
        copy.wait()
    left_freq = counts_ref[pairs_ref[0, pair]].astype(jnp.float32)
    right_freq = counts_ref[pairs_ref[1, pair]].astype(jnp.float32)
    group = 16 if per_device % 16 == 0 else per_device

    def values_of(first, block):
        rows, columns = slice(first, first + group), slice(block * LANES, (block + 1) * LANES)
        return [
            held[pair, who, kind, rows, columns].astype(jnp.float32)
            for who in (0, 1)
            for kind in (0, 1)
        ]

    for first in range(0, per_device, group):
        intersection = left_norm = right_norm = jnp.zeros((group, LANES), jnp.float32)
        for block in range(depth // LANES):
            left_gate, left_up, right_gate, right_up = values_of(first, block)
            intersection += left_gate * right_gate + left_up * right_up
            left_norm += left_gate * left_gate + left_up * left_up
            right_norm += right_gate * right_gate + right_up * right_up
        intersection, left_norm, right_norm = (
            jnp.sum(value, axis=1, keepdims=True) for value in (intersection, left_norm, right_norm)
        )
        similarity = (
            intersection
            * math.sqrt(2.0 * depth)
            / jnp.sqrt((left_norm + EPSILON) * (right_norm + EPSILON))
        )
        similarity_ref[0, first : first + group] = similarity
        share = right_freq * jax.nn.sigmoid(similarity)
        total = left_freq + share
        left_weight = jnp.broadcast_to(left_freq / total, (group, LANES))
        right_weight = jnp.broadcast_to(share / total, (group, LANES))
        for block in range(depth // LANES):
            left_gate, left_up, right_gate, right_up = values_of(first, block)
            woven[block, pl.ds(2 * first, group, stride=2), :] = (
                left_weight * left_gate + right_weight * right_gate
            )
            woven[block, pl.ds(2 * first + 1, group, stride=2), :] = (
                left_weight * left_up + right_weight * right_up
            )
    slot = lax.rem(pair, 2)

    def each_copy(which_pair, which_slot, act):
        for piece in range(pieces):
            index = which_pair * pieces + piece
            for where, parts in enumerate(targets):

                @pl.when(where_ref[index] == where)
                def _():
                    for part, (out_ref, begin) in enumerate(parts):
                        act(
                            pltpu.make_async_copy(
                                ready.at[which_slot, piece, :, pl.ds(begin, out_ref.shape[-1])],
                                out_ref.at[place_ref[index]],
                                sems.at[which_slot, piece, part],
                            )
                        )

    @pl.when(pair >= 2)
    def _():
        each_copy(pair - 2, slot, lambda copy: copy.wait())

    for block in range(depth // LANES):
        ready[slot, :, :, block * LANES : (block + 1) * LANES] = (
            woven[block].reshape(pieces, piece_rows, LANES).astype(jnp.bfloat16)
        )
    each_copy(pair, slot, lambda copy: copy.start())

    @pl.when(pair == pair_count - 1)
    def _():
        each_copy(pair - 1, 1 - slot, lambda copy: copy.wait())
        each_copy(pair, slot, lambda copy: copy.wait())


def merge(pairs, counts, where, places, rows, slots, listed):
    _, _, per_device, depth = rows.shape
    pair_count = pairs.shape[0]
    pieces = where.shape[0] // pair_count
    piece_rows = 2 * per_device // pieces
    shapes = [(slots, depth), (listed, depth), (listed, depth // 2), (listed, depth // 2), (listed, depth)]
    grid_spec = pltpu.PrefetchScalarGridSpec(
        num_scalar_prefetch=4,
        grid=(pair_count,),
        in_specs=[pl.BlockSpec(memory_space=pltpu.HBM)],
        out_specs=[pl.BlockSpec((1, per_device, 1), lambda p, *_: (p, 0, 0))]
        + [pl.BlockSpec(memory_space=pltpu.HBM)] * len(shapes),
        scratch_shapes=[
            pltpu.VMEM((pair_count, 2, 2, per_device, depth), jnp.bfloat16),
            pltpu.VMEM((depth // LANES, 2 * per_device, LANES), jnp.float32),
            pltpu.VMEM((2, pieces, piece_rows, depth), jnp.bfloat16),
            pltpu.SemaphoreType.DMA((pair_count, 2, 2)),
            pltpu.SemaphoreType.DMA((2, pieces, 2)),
        ],
    )
    return pl.pallas_call(
        merge_kernel,
        grid_spec=grid_spec,
        out_shape=[jax.ShapeDtypeStruct((pair_count, per_device, 1), jnp.float32)]
        + [
            jax.ShapeDtypeStruct((length, piece_rows, width), jnp.bfloat16)
            for length, width in shapes
        ],
        compiler_params=pltpu.CompilerParams(vmem_limit_bytes=VMEM),
        name="merge",
    )(pairs.T, counts, where, places, rows)


def place_three_kernel(filled_ref, quarters_ref, *refs):
    in_refs, out_ref = refs[:-1], refs[-1]
    slots, rows, _ = out_ref.shape
    count = rows // QUARTERS
    for slot in range(slots):
        keep = pl.program_id(0) * slots + slot < filled_ref[0]
        for index, in_ref in enumerate(in_refs):
            value = in_ref[:, slot].reshape(count, out_ref.shape[2])
            first = pl.multiple_of(quarters_ref[index] * count, count)
            out_ref[slot, pl.ds(first, count), :] = jnp.where(keep, value, jnp.zeros_like(value))


def place_three(filled, quarters, arrived):
    sources, cap, piece_rows, depth = arrived[0].shape
    slots = 2
    rows = QUARTERS * sources * piece_rows
    grid_spec = pltpu.PrefetchScalarGridSpec(
        num_scalar_prefetch=2,
        grid=(cap // slots,),
        in_specs=[pl.BlockSpec((sources, slots, piece_rows, depth), lambda s, *_: (0, s, 0, 0))]
        * len(arrived),
        out_specs=pl.BlockSpec((slots, rows, depth), lambda s, *_: (s, 0, 0)),
    )
    return pl.pallas_call(
        place_three_kernel,
        grid_spec=grid_spec,
        out_shape=jax.ShapeDtypeStruct((cap, rows, depth), arrived[0].dtype),
        compiler_params=pltpu.CompilerParams(vmem_limit_bytes=VMEM // 2),
        name="place_three",
    )(filled, quarters, *arrived)


def place_kernel(filled_ref, quarter_ref, in_ref, base_ref, out_ref):
    slots = out_ref.shape[0]
    for slot in range(slots):
        value = in_ref[:, slot].reshape(out_ref.shape[1:])
        keep = pl.program_id(0) * slots + slot < filled_ref[0]
        out_ref[slot] = jnp.where(keep, value, jnp.zeros_like(value))


def place(filled, quarter, arrived, part, base):
    sources, cap, piece_rows, width = arrived.shape
    slots = 2
    grid_spec = pltpu.PrefetchScalarGridSpec(
        num_scalar_prefetch=2,
        grid=(cap // slots,),
        in_specs=[
            pl.BlockSpec((sources, slots, piece_rows, width), lambda s, *_: (0, s, 0, 0)),
            pl.BlockSpec(memory_space=pltpu.HBM),
        ],
        out_specs=pl.BlockSpec(
            (slots, sources * piece_rows, width), lambda s, filled, quarter: (s, quarter[0], part)
        ),
    )
    return pl.pallas_call(
        place_kernel,
        grid_spec=grid_spec,
        out_shape=jax.ShapeDtypeStruct(base.shape, base.dtype),
        input_output_aliases={3: 0},
        compiler_params=pltpu.CompilerParams(vmem_limit_bytes=VMEM // 4),
        name="place",
    )(filled, quarter, arrived, base)


def body(gate_codes, up_codes, gate_scale, up_scale, pairs, counts, unit_order, owners):
    devices = lax.axis_size("expert")
    layers = lax.axis_size("layers")
    me = lax.axis_index("expert")
    units = gate_codes.shape[2]
    pieces = units // U
    share_units = U // devices
    size = devices // QUARTERS
    quarter = me // size
    pair_count = pairs.shape[0]
    all_pieces = pair_count * pieces

    owner_ids = owners[:, 0]
    owner_quarter = owner_ids // size
    earlier = jnp.arange(all_pieces)[None, :] < jnp.arange(all_pieces)[:, None]
    count_earlier = lambda values: jnp.sum(
        jnp.where((values[:, None] == values[None, :]) & earlier, 1, 0), axis=1
    ).astype(jnp.int32)
    slot = (owner_ids % size) * CAP + count_earlier(owner_ids)
    position = count_earlier(owner_quarter)
    where = (owner_quarter - quarter + QUARTERS) % QUARTERS
    places = jnp.where(where == 0, slot, position)
    filled = jnp.sum((owner_ids == me).astype(jnp.int32))[None]
    from_list = jnp.sum(
        jnp.where(
            (jnp.arange(size * CAP)[:, None] == slot[None, :]) & (where == 0)[None, :],
            position[None, :],
            0,
        ),
        axis=1,
    ).astype(jnp.int32)
    here = (jnp.max(position) + 1).astype(jnp.int32)
    longest = here
    for shift in range(1, layers):
        ring = [(layer, (layer + shift) % layers) for layer in range(layers)]
        longest = jnp.maximum(longest, lax.ppermute(here, "layers", ring))
    least = all_pieces // QUARTERS
    lengths = sorted({min(size * CAP, -(-least * part // 12)) for part in LIST_PARTS})
    any_piece = longest > 0
    level = sum((longest > length).astype(jnp.int32) for length in lengths[:-1])

    outgoing = prepare(
        pairs, me, unit_order, gate_codes[0], up_codes[0], gate_scale[0].T, up_scale[0].T, devices
    )
    rows = lax.all_to_all(outgoing, "expert", split_axis=0, concat_axis=0, tiled=True)

    groups = [list(range(first, first + size)) for first in range(0, devices, size)]

    def within_quarter(value):
        value = value.reshape(size, CAP, value.shape[1], value.shape[2])
        return lax.all_to_all(
            value, "expert", split_axis=0, concat_axis=0, tiled=True, axis_index_groups=groups
        )

    def deal(listed, rows, where, places, from_list, any_piece):
        similarity_part, slots, next_list, far_first, far_second, last_list = merge(
            pairs, counts, where, places, rows, size * CAP, listed
        )
        origins = jnp.stack([(quarter - shift + QUARTERS) % QUARTERS for shift in range(QUARTERS)])
        origins = origins.astype(jnp.int32)

        def permuted(chunk, shift):
            ring = [(device, (device + shift * size) % devices) for device in range(devices)]
            return lax.ppermute(chunk, "expert", ring)

        def in_order(*values):
            return lax.optimization_barrier(values)

        def unless_empty(exchange, *values):
            shapes = jax.eval_shape(exchange, *values)
            zeros = lambda *_: jax.tree.map(lambda v: jnp.zeros(v.shape, v.dtype), shapes)
            return lax.cond(any_piece, exchange, zeros, *values)

        def spread(chunk, from_list):
            return within_quarter(jnp.take(chunk, from_list, axis=0, mode="clip"))

        def spread_and_place(chunk, from_list, filled, quarters, *arrived):
            return spread(chunk, from_list), place_three(filled, quarters, arrived)

        one_on = permuted(next_list, 1)
        own = unless_empty(within_quarter, slots)
        one_on, own = in_order(one_on, own)
        last_list, _ = in_order(last_list, one_on)
        three_on = permuted(last_list, 3)
        from_one = unless_empty(spread, one_on, from_list)
        three_on, from_one = in_order(three_on, from_one)
        far_first, _ = in_order(far_first, three_on)
        two_on = permuted(far_first, 2)
        from_three = unless_empty(spread, three_on, from_list)
        two_on, from_three = in_order(two_on, from_three)
        far_second, _ = in_order(far_second, two_on)
        rest_on = permuted(far_second, 2)
        from_two, merged = unless_empty(
            spread_and_place,
            two_on,
            from_list,
            filled,
            origins[jnp.array([0, 1, 3])],
            own,
            from_one,
            from_three,
        )
        part, from_two = in_order(similarity_part.reshape(1, -1), from_two)
        similarity = lax.all_to_all(
            jnp.broadcast_to(part, (devices, part.shape[1])), "expert", 0, 0, tiled=True
        )
        rest_on, similarity = in_order(rest_on, similarity)
        from_rest = spread(rest_on, from_list)
        merged = place(filled, origins[2:3], from_two, 0, merged)
        merged = place(filled, origins[2:3], from_rest, 1, merged)
        similarity = similarity.reshape(devices, pair_count, pieces, share_units)
        similarity = similarity.transpose(1, 2, 0, 3).reshape(pair_count, units)
        return merged, similarity

    return lax.switch(
        level,
        [functools.partial(deal, length) for length in lengths],
        rows,
        where,
        places,
        from_list,
        any_piece,
    )


def solution(mesh):
    in_specs = (
        P(("layers", "expert"), None, None),
        P(("layers", "expert"), None, None),
        P(("layers", "expert"), None, None),
        P(("layers", "expert"), None, None),
        P("layers", None),
        P("layers"),
        P("layers", None),
        P("layers", None),
    )
    out_specs = (P(("layers", "expert"), None, None), P("layers", None))
    return jax.shard_map(body, mesh=mesh, in_specs=in_specs, out_specs=out_specs, check_vma=False)
```

```python
import functools
import math

import jax
import jax.numpy as jnp
from jax import lax
from jax.experimental import pallas as pl
from jax.experimental.pallas import tpu as pltpu
from jax.sharding import PartitionSpec as P

BLK = 128
U = 128
LANES = 128
CAP = 6
EPSILON = 1e-06
VMEM = 60 * 1024 * 1024
QUARTERS = 4
LIST_PARTS = (15, 16, 17, 18, 19, 20, 24)


def prepare_kernel(
    pairs_ref, me_ref, order_ref, gate_ref, up_ref, gate_scale_ref, up_scale_ref, out_ref, select_ref, scale_ref
):
    units = select_ref.shape[1]
    tile = gate_ref.shape[0]
    devices, _, per_device, _ = out_ref.shape
    step = pl.program_id(0)

    @pl.when(step == 0)
    def _():
        order = lax.broadcasted_iota(jnp.int32, (1, units), 1)
        for pair in range(order_ref.shape[0]):
            order = jnp.where(
                pairs_ref[1, pair] == me_ref[0], order_ref[pair : pair + 1, :], order
            )
        share = U // devices
        columns = lax.broadcasted_iota(jnp.int32, (1, units), 1)
        matched = order.astype(jnp.float32)
        group = 16
        for first in range(0, units, group):
            row = first + lax.broadcasted_iota(jnp.int32, (group, 1), 0)
            device = lax.div(row, per_device)
            within = row - device * per_device
            piece = lax.div(within, share)
            unit = piece * U + device * share + within - piece * share
            source = jnp.sum(
                jnp.where(unit == columns, matched, 0.0), axis=1, keepdims=True
            ).astype(jnp.int32)
            select_ref[first : first + group] = (
                (source == columns).astype(jnp.float32).astype(jnp.bfloat16)
            )
        for kind, scales in enumerate((gate_scale_ref, up_scale_ref)):
            blocks = scales.shape[0]
            block = lax.broadcasted_iota(jnp.int32, (blocks, units), 0)
            column = lax.broadcasted_iota(jnp.int32, (blocks, units), 1)
            covers = (lax.div(column, BLK) == block).astype(jnp.float32).astype(jnp.bfloat16)
            scale_ref[kind] = lax.dot_general(
                scales[...], covers, (((0,), (0,)), ((), ())), preferred_element_type=jnp.float32
            )

    for kind, codes_ref in enumerate((gate_ref, up_ref)):
        parts = []
        for block in range(tile // BLK):
            scale = scale_ref[kind, pl.ds(step * (tile // BLK) + block, 1), :].astype(jnp.bfloat16)
            parts.append(codes_ref[block * BLK : (block + 1) * BLK, :] * scale)
        values = jnp.concatenate(parts, axis=0)
        chosen = lax.dot_general(
            select_ref[...], values, (((1,), (1,)), ((), ())), preferred_element_type=jnp.float32
        ).astype(jnp.bfloat16)
        out_ref[:, kind] = chosen.reshape(devices, per_device, tile)


def prepare(pairs, me, unit_order, gate_codes, up_codes, gate_scale, up_scale, devices):
    depth, units = gate_codes.shape
    per_device = units // devices
    tile = 512
    whole = lambda array: pl.BlockSpec(array.shape, lambda d, *_: (0, 0))
    grid_spec = pltpu.PrefetchScalarGridSpec(
        num_scalar_prefetch=2,
        grid=(depth // tile,),
        in_specs=[
            whole(unit_order),
            pl.BlockSpec((tile, units), lambda d, *_: (d, 0)),
            pl.BlockSpec((tile, units), lambda d, *_: (d, 0)),
            whole(gate_scale),
            whole(up_scale),
        ],
        out_specs=pl.BlockSpec((devices, 2, per_device, tile), lambda d, *_: (0, 0, 0, d)),
        scratch_shapes=[
            pltpu.VMEM((units, units), jnp.bfloat16),
            pltpu.VMEM((2, depth // BLK, units), jnp.float32),
        ],
    )
    return pl.pallas_call(
        prepare_kernel,
        grid_spec=grid_spec,
        out_shape=jax.ShapeDtypeStruct((devices, 2, per_device, depth), jnp.bfloat16),
        compiler_params=pltpu.CompilerParams(vmem_limit_bytes=VMEM),
        name="prepare",
    )(pairs.T, me[None], unit_order, gate_codes, up_codes, gate_scale, up_scale)


def merge_kernel(
    pairs_ref, counts_ref, where_ref, place_ref, rows_ref, similarity_ref, *rest
):
    outs, (held, woven, ready, arrive, sems) = rest[:-5], rest[-5:]
    pair = pl.program_id(0)
    pair_count = pl.num_programs(0)
    per_device, depth = held.shape[3], held.shape[4]
    pieces, piece_rows = ready.shape[1], ready.shape[2]
    targets = (
        [(outs[0], 0)],
        [(outs[1], 0)],
        [(outs[2], 0), (outs[3], depth // 2)],
        [(outs[4], 0)],
    )

    def fetches(which_pair):
        return [
            pltpu.make_async_copy(
                rows_ref.at[pairs_ref[who, which_pair], kind],
                held.at[which_pair, who, kind],
                arrive.at[which_pair, who, kind],
            )
            for who in (0, 1)
            for kind in (0, 1)
        ]

    @pl.when(pair == 0)
    def _():
        @pl.loop(0, held.shape[0])
        def _(which_pair):
            for copy in fetches(which_pair):
                copy.start()

    for copy in fetches(pair):
        copy.wait()
    left_freq = counts_ref[pairs_ref[0, pair]].astype(jnp.float32)
    right_freq = counts_ref[pairs_ref[1, pair]].astype(jnp.float32)
    group = 16 if per_device % 16 == 0 else per_device

    def values_of(first, block):
        rows, columns = slice(first, first + group), slice(block * LANES, (block + 1) * LANES)
        return [
            held[pair, who, kind, rows, columns].astype(jnp.float32)
            for who in (0, 1)
            for kind in (0, 1)
        ]

    for first in range(0, per_device, group):
        intersection = left_norm = right_norm = jnp.zeros((group, LANES), jnp.float32)
        for block in range(depth // LANES):
            left_gate, left_up, right_gate, right_up = values_of(first, block)
            intersection += left_gate * right_gate + left_up * right_up
            left_norm += left_gate * left_gate + left_up * left_up
            right_norm += right_gate * right_gate + right_up * right_up
        intersection, left_norm, right_norm = (
            jnp.sum(value, axis=1, keepdims=True) for value in (intersection, left_norm, right_norm)
        )
        similarity = (
            intersection
            * math.sqrt(2.0 * depth)
            / jnp.sqrt((left_norm + EPSILON) * (right_norm + EPSILON))
        )
        similarity_ref[0, first : first + group] = similarity
        share = right_freq * jax.nn.sigmoid(similarity)
        total = left_freq + share
        left_weight = jnp.broadcast_to(left_freq / total, (group, LANES))
        right_weight = jnp.broadcast_to(share / total, (group, LANES))
        for block in range(depth // LANES):
            left_gate, left_up, right_gate, right_up = values_of(first, block)
            woven[block, pl.ds(2 * first, group, stride=2), :] = (
                left_weight * left_gate + right_weight * right_gate
            )
            woven[block, pl.ds(2 * first + 1, group, stride=2), :] = (
                left_weight * left_up + right_weight * right_up
            )
    slot = lax.rem(pair, 2)

    def each_copy(which_pair, which_slot, act):
        for piece in range(pieces):
            index = which_pair * pieces + piece
            for where, parts in enumerate(targets):

                @pl.when(where_ref[index] == where)
                def _():
                    for part, (out_ref, begin) in enumerate(parts):
                        act(
                            pltpu.make_async_copy(
                                ready.at[which_slot, piece, :, pl.ds(begin, out_ref.shape[-1])],
                                out_ref.at[place_ref[index]],
                                sems.at[which_slot, piece, part],
                            )
                        )

    @pl.when(pair >= 2)
    def _():
        each_copy(pair - 2, slot, lambda copy: copy.wait())

    for block in range(depth // LANES):
        ready[slot, :, :, block * LANES : (block + 1) * LANES] = (
            woven[block].reshape(pieces, piece_rows, LANES).astype(jnp.bfloat16)
        )
    each_copy(pair, slot, lambda copy: copy.start())

    @pl.when(pair == pair_count - 1)
    def _():
        each_copy(pair - 1, 1 - slot, lambda copy: copy.wait())
        each_copy(pair, slot, lambda copy: copy.wait())


def merge(pairs, counts, where, places, rows, slots, listed):
    _, _, per_device, depth = rows.shape
    pair_count = pairs.shape[0]
    pieces = where.shape[0] // pair_count
    piece_rows = 2 * per_device // pieces
    shapes = [(slots, depth), (listed, depth), (listed, depth // 2), (listed, depth // 2), (listed, depth)]
    grid_spec = pltpu.PrefetchScalarGridSpec(
        num_scalar_prefetch=4,
        grid=(pair_count,),
        in_specs=[pl.BlockSpec(memory_space=pltpu.HBM)],
        out_specs=[pl.BlockSpec((1, per_device, 1), lambda p, *_: (p, 0, 0))]
        + [pl.BlockSpec(memory_space=pltpu.HBM)] * len(shapes),
        scratch_shapes=[
            pltpu.VMEM((pair_count, 2, 2, per_device, depth), jnp.bfloat16),
            pltpu.VMEM((depth // LANES, 2 * per_device, LANES), jnp.float32),
            pltpu.VMEM((2, pieces, piece_rows, depth), jnp.bfloat16),
            pltpu.SemaphoreType.DMA((pair_count, 2, 2)),
            pltpu.SemaphoreType.DMA((2, pieces, 2)),
        ],
    )
    return pl.pallas_call(
        merge_kernel,
        grid_spec=grid_spec,
        out_shape=[jax.ShapeDtypeStruct((pair_count, per_device, 1), jnp.float32)]
        + [
            jax.ShapeDtypeStruct((length, piece_rows, width), jnp.bfloat16)
            for length, width in shapes
        ],
        compiler_params=pltpu.CompilerParams(vmem_limit_bytes=VMEM),
        name="merge",
    )(pairs.T, counts, where, places, rows)


def place_three_kernel(filled_ref, quarters_ref, *refs):
    in_refs, out_ref = refs[:-1], refs[-1]
    slots, rows, _ = out_ref.shape
    count = rows // QUARTERS
    for slot in range(slots):
        keep = pl.program_id(0) * slots + slot < filled_ref[0]
        for index, in_ref in enumerate(in_refs):
            value = in_ref[:, slot].reshape(count, out_ref.shape[2])
            first = pl.multiple_of(quarters_ref[index] * count, count)
            out_ref[slot, pl.ds(first, count), :] = jnp.where(keep, value, jnp.zeros_like(value))


def place_three(filled, quarters, arrived):
    sources, cap, piece_rows, depth = arrived[0].shape
    slots = 2
    rows = QUARTERS * sources * piece_rows
    grid_spec = pltpu.PrefetchScalarGridSpec(
        num_scalar_prefetch=2,
        grid=(cap // slots,),
        in_specs=[pl.BlockSpec((sources, slots, piece_rows, depth), lambda s, *_: (0, s, 0, 0))]
        * len(arrived),
        out_specs=pl.BlockSpec((slots, rows, depth), lambda s, *_: (s, 0, 0)),
    )
    return pl.pallas_call(
        place_three_kernel,
        grid_spec=grid_spec,
        out_shape=jax.ShapeDtypeStruct((cap, rows, depth), arrived[0].dtype),
        compiler_params=pltpu.CompilerParams(vmem_limit_bytes=VMEM // 2),
        name="place_three",
    )(filled, quarters, *arrived)


def place_kernel(filled_ref, quarter_ref, in_ref, base_ref, out_ref):
    slots = out_ref.shape[0]
    for slot in range(slots):
        value = in_ref[:, slot].reshape(out_ref.shape[1:])
        keep = pl.program_id(0) * slots + slot < filled_ref[0]
        out_ref[slot] = jnp.where(keep, value, jnp.zeros_like(value))


def place(filled, quarter, arrived, part, base):
    sources, cap, piece_rows, width = arrived.shape
    slots = 2
    grid_spec = pltpu.PrefetchScalarGridSpec(
        num_scalar_prefetch=2,
        grid=(cap // slots,),
        in_specs=[
            pl.BlockSpec((sources, slots, piece_rows, width), lambda s, *_: (0, s, 0, 0)),
            pl.BlockSpec(memory_space=pltpu.HBM),
        ],
        out_specs=pl.BlockSpec(
            (slots, sources * piece_rows, width), lambda s, filled, quarter: (s, quarter[0], part)
        ),
    )
    return pl.pallas_call(
        place_kernel,
        grid_spec=grid_spec,
        out_shape=jax.ShapeDtypeStruct(base.shape, base.dtype),
        input_output_aliases={3: 0},
        compiler_params=pltpu.CompilerParams(vmem_limit_bytes=VMEM // 4),
        name="place",
    )(filled, quarter, arrived, base)


def body(gate_codes, up_codes, gate_scale, up_scale, pairs, counts, unit_order, owners):
    devices = lax.axis_size("expert")
    layers = lax.axis_size("layers")
    me = lax.axis_index("expert")
    units = gate_codes.shape[2]
    pieces = units // U
    share_units = U // devices
    size = devices // QUARTERS
    quarter = me // size
    pair_count = pairs.shape[0]
    all_pieces = pair_count * pieces

    owner_ids = owners[:, 0]
    owner_quarter = owner_ids // size
    earlier = jnp.arange(all_pieces)[None, :] < jnp.arange(all_pieces)[:, None]
    count_earlier = lambda values: jnp.sum(
        jnp.where((values[:, None] == values[None, :]) & earlier, 1, 0), axis=1
    ).astype(jnp.int32)
    slot = (owner_ids % size) * CAP + count_earlier(owner_ids)
    position = count_earlier(owner_quarter)
    where = (owner_quarter - quarter + QUARTERS) % QUARTERS
    places = jnp.where(where == 0, slot, position)
    filled = jnp.sum((owner_ids == me).astype(jnp.int32))[None]
    from_list = jnp.sum(
        jnp.where(
            (jnp.arange(size * CAP)[:, None] == slot[None, :]) & (where == 0)[None, :],
            position[None, :],
            0,
        ),
        axis=1,
    ).astype(jnp.int32)
    here = (jnp.max(position) + 1).astype(jnp.int32)
    longest = here
    for shift in range(1, layers):
        ring = [(layer, (layer + shift) % layers) for layer in range(layers)]
        longest = jnp.maximum(longest, lax.ppermute(here, "layers", ring))
    least = all_pieces // QUARTERS
    lengths = sorted({min(size * CAP, -(-least * part // 12)) for part in LIST_PARTS})
    any_piece = longest > 0
    level = sum((longest > length).astype(jnp.int32) for length in lengths[:-1])

    outgoing = prepare(
        pairs, me, unit_order, gate_codes[0], up_codes[0], gate_scale[0].T, up_scale[0].T, devices
    )
    rows = lax.all_to_all(outgoing, "expert", split_axis=0, concat_axis=0, tiled=True)

    groups = [list(range(first, first + size)) for first in range(0, devices, size)]

    def within_quarter(value):
        value = value.reshape(size, CAP, value.shape[1], value.shape[2])
        return lax.all_to_all(
            value, "expert", split_axis=0, concat_axis=0, tiled=True, axis_index_groups=groups
        )

    def deal(listed, rows, where, places, from_list, any_piece):
        similarity_part, slots, next_list, far_first, far_second, last_list = merge(
            pairs, counts, where, places, rows, size * CAP, listed
        )
        origins = jnp.stack([(quarter - shift + QUARTERS) % QUARTERS for shift in range(QUARTERS)])
        origins = origins.astype(jnp.int32)

        def permuted(chunk, shift):
            ring = [(device, (device + shift * size) % devices) for device in range(devices)]
            return lax.ppermute(chunk, "expert", ring)

        def in_order(*values):
            return lax.optimization_barrier(values)

        def unless_empty(exchange, *values):
            shapes = jax.eval_shape(exchange, *values)
            zeros = lambda *_: jax.tree.map(lambda v: jnp.zeros(v.shape, v.dtype), shapes)
            return lax.cond(any_piece, exchange, zeros, *values)

        def spread(chunk, from_list):
            return within_quarter(jnp.take(chunk, from_list, axis=0, mode="clip"))

        def spread_and_place(chunk, from_list, filled, quarters, *arrived):
            return spread(chunk, from_list), place_three(filled, quarters, arrived)

        one_on = permuted(next_list, 1)
        own = unless_empty(within_quarter, slots)
        one_on, own = in_order(one_on, own)
        last_list, _ = in_order(last_list, one_on)
        three_on = permuted(last_list, 3)
        from_one = unless_empty(spread, one_on, from_list)
        three_on, from_one = in_order(three_on, from_one)
        far_first, _ = in_order(far_first, three_on)
        two_on = permuted(far_first, 2)
        from_three = unless_empty(spread, three_on, from_list)
        two_on, from_three = in_order(two_on, from_three)
        far_second, _ = in_order(far_second, two_on)
        rest_on = permuted(far_second, 2)
        from_two, merged = unless_empty(
            spread_and_place,
            two_on,
            from_list,
            filled,
            origins[jnp.array([0, 1, 3])],
            own,
            from_one,
            from_three,
        )
        part, from_two = in_order(similarity_part.reshape(1, -1), from_two)
        similarity = lax.all_to_all(
            jnp.broadcast_to(part, (devices, part.shape[1])), "expert", 0, 0, tiled=True
        )
        from_rest = spread(rest_on, from_list)
        merged = place(filled, origins[2:3], from_two, 0, merged)
        merged = place(filled, origins[2:3], from_rest, 1, merged)
        similarity = similarity.reshape(devices, pair_count, pieces, share_units)
        similarity = similarity.transpose(1, 2, 0, 3).reshape(pair_count, units)
        return merged, similarity

    return lax.switch(
        level,
        [functools.partial(deal, length) for length in lengths],
        rows,
        where,
        places,
        from_list,
        any_piece,
    )


def solution(mesh):
    in_specs = (
        P(("layers", "expert"), None, None),
        P(("layers", "expert"), None, None),
        P(("layers", "expert"), None, None),
        P(("layers", "expert"), None, None),
        P("layers", None),
        P("layers"),
        P("layers", None),
        P("layers", None),
    )
    out_specs = (P(("layers", "expert"), None, None), P("layers", None))
    return jax.shard_map(body, mesh=mesh, in_specs=in_specs, out_specs=out_specs, check_vma=False)
```
